32 devices in a mesh: blk: 4 (over z), bank: 8 (over y, x, core).
Axes of the slice: x: 2, y: 2, z: 4, core: 2. Of those that a mesh axis runs over, the one named last changes fastest.
Arguments:
- log_density: bfloat16 [128, 32768], P(('blk', 'bank')), may hold values from -8 to 8
- assignment: int32 [128], P(('blk', 'bank')), may hold values from 0 to 7, as said below
Outputs:
- centers: bfloat16 [8, 32768], P(None, 'bank')
- potentials: float32 [128, 32768], P(('blk', 'bank'))
The draws below stay inside these ranges and needn't reach their ends.
Inputs may be any that keep to these rules, and one draw needn't show every extreme that they name: Every barycenter index is the assignment of at least one member.
All inputs are finite; a program needn't handle non-finite values.
Results may differ from the reference program's by a relative error of at most 0.0051.
Values may be sent and summed in bfloat16 or wider, within the bound.
A program may use at most 64 MiB of HBM per device.

```python
import jax
import jax.numpy as jnp
from jax import lax

G = 32
M_DEV = 4
BARS = 8
ITERS = 2
CELLS = 32768
MEMBERS = 128


def draw_assignment(key, part):
    key_order, key_rare, key_first, key_second, key_roll = jax.random.split(key, 5)
    order = jax.random.permutation(key_order, BARS)
    rare_count = BARS // 2
    rare_pick = jax.random.randint(key_rare, (MEMBERS,), 0, rare_count)
    first_pick = jax.random.randint(key_first, (MEMBERS,), rare_count, BARS)
    second_pick = jax.random.randint(key_second, (MEMBERS,), rare_count, BARS)
    common_pick = jnp.minimum(first_pick, second_pick)
    roll = jax.random.randint(key_roll, (MEMBERS,), 0, MEMBERS)
    ranked = jnp.where(roll < 2 * BARS, rare_pick, common_pick)
    member_index = jnp.arange(MEMBERS, dtype=jnp.int32)
    ranked = jnp.where(member_index < BARS, member_index, ranked)
    return order[ranked].astype(jnp.int32)


def block_scale(key, shape, cuts, low, largest):
    level, own = 1.0, jax.random.fold_in(key, 6)
    for axis_at, shards_of in cuts:
        steps = jnp.exp(jax.random.uniform(jax.random.fold_in(own, axis_at), (shards_of,), jnp.float32, low / len(cuts), largest / len(cuts)))
        level = level * jnp.repeat(steps, shape[axis_at] // shards_of).reshape([-1 if axis == axis_at else 1 for axis in range(len(shape))])
    return level


def noise(stream_key, dims, scale, most, cuts=(), kind=jnp.bfloat16):
    result = scale * jax.random.normal(stream_key, dims, jnp.float32)
    if cuts:
        result = result * block_scale(stream_key, dims, cuts, -0.22, 0.18)
    return jnp.clip(result, -most, most).astype(kind)


def setup_inputs(seed: int = 0) -> dict:
    splits = jax.random.split(jax.random.key(seed), 3)
    return {
        "log_density": noise(splits[0], (MEMBERS, CELLS), 2.0, 8.0, ((0, 32),)),
        "assignment": draw_assignment(jax.random.fold_in(splits[2], 71), 0),
    }


def kernel_tables():
    grid_pos = jnp.arange(G, dtype=jnp.float32)
    offset = grid_pos[:, None] - grid_pos[None, :]
    kernel_line = jnp.exp(-0.5 * offset * offset)
    kernel_pair = (kernel_line[:, None, :, None] * kernel_line[None, :, None, :]).reshape(G * G, G * G).astype(jnp.bfloat16)
    return kernel_line, kernel_pair


def log_convolve(field_log, kernel_line, kernel_pair):
    member_count = field_log.shape[0]
    raised = jnp.exp(field_log).astype(jnp.bfloat16).reshape(member_count * G, G * G)
    inner_sum = jnp.dot(raised, kernel_pair, preferred_element_type=jnp.float32).reshape(member_count, G, G * G)
    outer_sum = jnp.einsum("ij,mjc->mic", kernel_line, inner_sum, precision=lax.Precision.HIGHEST)
    return jnp.log(outer_sum).reshape(member_count, G * G * G)


def reference(log_density, assignment):
    kernel_line, kernel_pair = kernel_tables()
    labels = jnp.arange(BARS, dtype=jnp.int32)
    onehot = (assignment[:, None] == labels[None, :]).astype(jnp.float32)
    counts = jnp.sum(onehot, axis=0)
    groups = MEMBERS // M_DEV
    density_blocks = log_density.reshape(groups, M_DEV, CELLS)
    onehot_blocks = onehot.reshape(groups, M_DEV, BARS)
    potential = jnp.zeros((groups, M_DEV, CELLS), jnp.float32)
    centers = jnp.zeros((BARS, CELLS), jnp.bfloat16)
    for iteration in range(ITERS):
        def member_side(packed):
            density, scaling = packed
            source = density.astype(jnp.float32) - log_convolve(scaling, kernel_line, kernel_pair)
            return log_convolve(source, kernel_line, kernel_pair)
        smoothed = lax.map(member_side, (density_blocks, potential))
        sums = jnp.einsum("gmk,gmc->kc", onehot_blocks, smoothed, precision=lax.Precision.HIGHEST)
        centers = (sums / counts[:, None]).astype(jnp.bfloat16)
        chosen = jnp.einsum("gmk,kc->gmc", onehot_blocks, centers.astype(jnp.float32), precision=lax.Precision.HIGHEST)
        potential = chosen - smoothed
    return centers, potential.reshape(MEMBERS, CELLS)
```

```python
import functools

import jax
import jax.numpy as jnp
import ml_dtypes
import numpy as np
from jax import lax
from jax.experimental import pallas as pl
from jax.experimental.pallas import tpu as pltpu
from jax.sharding import PartitionSpec as P

G = 32
PLANE = G * G
BARS = 8
ITERS = 2
MESH = pl.DeviceIdType.MESH
F32 = jnp.float32
BF16 = jnp.bfloat16


def host_tables():
    grid_pos = np.arange(G, dtype=np.float32)
    offset = grid_pos[:, None] - grid_pos[None, :]
    line = np.exp(np.float32(-0.5) * offset * offset)
    pair = (line[:, None, :, None] * line[None, :, None, :]).reshape(PLANE, PLANE).astype(ml_dtypes.bfloat16)
    return line, pair


def kernel(
    groups, banks, members,
    density_ref, label_ref, pair_hbm, line_ref, row_ref, column_ref,
    centers_ref, potential_ref,
    pair, raised, source, lifted, smoothed, outgoing, incoming, partial, partial_in, shared, chosen, chosen_in,
    labels, label_out, count_out, count_in,
    pair_sem, label_sem, count_sem, member_send, member_recv, partial_sem, shared_send, shared_recv, chosen_send, chosen_recv,
):
    blk, bank = lax.axis_index("blk"), lax.axis_index("bank")
    rows = G * members
    chunk = rows // banks
    slabs = G // banks
    width = PLANE // groups
    kept = slabs * BARS

    def group_at(step):
        return lax.rem(blk + step, groups)

    def bank_at(step):
        return lax.rem(bank + step, banks)

    def chunk_at(index):
        return pl.ds(pl.multiple_of(index * chunk, chunk), chunk)

    def push(src, dst, send_sem, recv_sem, device):
        pltpu.make_async_remote_copy(
            src_ref=src, dst_ref=dst, send_sem=send_sem, recv_sem=recv_sem,
            device_id=device, device_id_type=MESH,
        ).start()

    def await_bytes(ref, sem):
        pltpu.make_async_copy(ref, ref, sem).wait()

    load_pair = pltpu.make_async_copy(pair_hbm, pair, pair_sem)
    load_pair.start()
    barrier = pltpu.get_barrier_semaphore()
    for step in range(1, banks):
        pl.semaphore_signal(barrier, inc=1, device_id=(blk, bank_at(step)), device_id_type=MESH)
    for step in range(1, groups):
        pl.semaphore_signal(barrier, inc=1, device_id=(group_at(step), bank), device_id_type=MESH)

    own_rows = lax.broadcasted_iota(jnp.int32, (chunk, 128), 0) % members
    own_labels = jnp.zeros((chunk, 128), F32)
    for member in range(members):
        own_labels = jnp.where(own_rows == member, label_ref[member].astype(F32), own_labels)
    label_out[...] = own_labels.astype(BF16)
    labels[chunk_at(bank), :] = own_labels.astype(BF16)

    for tile in range(groups):
        for x in range(G):
            lifted[tile, members * x:members * (x + 1), :] = density_ref[
                :, x * PLANE + tile * width:x * PLANE + (tile + 1) * width
            ].astype(F32)
    for tile in range(groups):
        risen = jnp.exp(lifted[tile])
        lifted[tile] = risen
        columns = slice(tile * width, (tile + 1) * width)
        source[:, columns] = (risen * (row_ref[...] * column_ref[:, columns])).astype(BF16)

    pl.semaphore_wait(barrier, banks - 1 + groups - 1)
    for step in range(1, banks):
        push(label_out, labels.at[chunk_at(bank), :], label_sem.at[0], label_sem.at[1], (blk, bank_at(step)))
    load_pair.wait()

    def convolve(field, tile):
        inner = jnp.dot(field, pair[tile], preferred_element_type=F32)
        return jnp.dot(line_ref[...], inner, precision=lax.Precision.HIGHEST, preferred_element_type=F32)

    pick = None
    for iteration in range(ITERS):
        last = iteration == ITERS - 1
        if iteration:
            for tile in range(groups):
                source[:, tile * width:(tile + 1) * width] = (lifted[tile] / convolve(raised[...], tile)).astype(BF16)

        for step in range(1, groups + 1):
            tile = group_at(step)
            value = jnp.log(convolve(source[...], tile))
            smoothed[tile] = value
            outgoing[iteration, tile] = value.astype(BF16)
            incoming[iteration, tile, chunk_at(bank), :] = outgoing[iteration, tile, chunk_at(bank), :]
            for hop in range(1, banks):
                peer = bank_at(hop)
                push(
                    outgoing.at[iteration, tile, chunk_at(peer), :],
                    incoming.at[iteration, tile, chunk_at(bank), :],
                    member_send.at[iteration], member_recv.at[iteration, tile], (blk, peer),
                )

        if iteration == 0:
            await_bytes(labels.at[0:rows - chunk, :], label_sem.at[1])
            row = lax.broadcasted_iota(jnp.int32, (rows, 128), 0)
            lane = lax.broadcasted_iota(jnp.int32, (rows, 128), 1)
            match = (labels[...].astype(F32) == (lane % BARS).astype(F32)) & ((row // members) % slabs == lane // BARS)
            pick_wide = jnp.where(match, 1.0, 0.0).astype(F32)
            gather_wide = jnp.transpose(pick_wide)
            pick = pick_wide.astype(BF16)[:, :kept]
            gather = gather_wide.astype(BF16)[:kept, :]
            own_count = jnp.broadcast_to(jnp.sum(gather_wide[:BARS, :], axis=1, keepdims=True), (BARS, 128))
            count_out[...] = own_count
            count_in[blk] = own_count
            for step in range(1, groups):
                push(count_out, count_in.at[blk], count_sem.at[0], count_sem.at[1], (group_at(step), bank))

        for step in range(1, groups + 1):
            tile = group_at(step)
            await_bytes(incoming.at[iteration, tile, 0:rows - chunk, :], member_recv.at[iteration, tile])
            sums = jnp.dot(gather, incoming[iteration, tile], preferred_element_type=F32)
            if step < groups:
                partial[iteration, tile] = sums
                push(
                    partial.at[iteration, tile], partial_in.at[iteration, blk],
                    partial_sem.at[iteration, 0], partial_sem.at[iteration, 1], (tile, bank),
                )
            else:
                partial_in[iteration, blk] = sums

        if iteration == 0:
            await_bytes(count_in.at[0:groups - 1], count_sem.at[1])
            counts = functools.reduce(jnp.add, [count_in[group] for group in range(groups)])
            counts = jnp.concatenate([counts[:, :1]] * slabs, axis=0)
        await_bytes(partial_in.at[iteration, 0:groups - 1], partial_sem.at[iteration, 1])
        total = functools.reduce(jnp.add, [partial_in[iteration, group] for group in range(groups)])
        shared[iteration, blk] = (total / counts).astype(BF16)
        for step in range(1, groups):
            push(
                shared.at[iteration, blk], shared.at[iteration, blk],
                shared_send.at[iteration], shared_recv.at[iteration, blk], (group_at(step), bank),
            )

        for step in range(groups):
            tile = group_at(step)
            if step:
                await_bytes(shared.at[iteration, tile], shared_recv.at[iteration, tile])
            center = shared[iteration, tile]
            chosen[iteration, tile] = jnp.dot(pick, center, preferred_element_type=F32).astype(BF16)
            chosen_in[iteration, tile, chunk_at(bank), :] = chosen[iteration, tile, chunk_at(bank), :]
            for hop in range(1, banks):
                peer = bank_at(hop)
                push(
                    chosen.at[iteration, tile, chunk_at(peer), :],
                    chosen_in.at[iteration, tile, chunk_at(bank), :],
                    chosen_send.at[iteration], chosen_recv.at[iteration, tile], (blk, peer),
                )
            if last:
                for slab in range(slabs):
                    start = pl.multiple_of(slab * PLANE + tile * width, width)
                    centers_ref[:, pl.ds(start, width)] = center[slab * BARS:(slab + 1) * BARS, :]

        for step in range(groups):
            tile = group_at(step)
            await_bytes(chosen_in.at[iteration, tile, 0:rows - chunk, :], chosen_recv.at[iteration, tile])
            value = chosen_in[iteration, tile].astype(F32) - smoothed[tile]
            if last:
                for x in range(G):
                    start = pl.multiple_of(x * PLANE + tile * width, width)
                    potential_ref[:, pl.ds(start, width)] = value[members * x:members * (x + 1), :]
            else:
                raised[:, pl.ds(pl.multiple_of(tile * width, width), width)] = jnp.exp(value).astype(BF16)

    for _ in range(banks - 1):
        await_bytes(label_out, label_sem.at[0])
    for _ in range(groups - 1):
        await_bytes(count_out, count_sem.at[0])
    for iteration in range(ITERS):
        await_bytes(outgoing.at[iteration, :, 0:rows - chunk, :], member_send.at[iteration])
        await_bytes(partial.at[iteration, 0:groups - 1], partial_sem.at[iteration, 0])
        await_bytes(shared.at[iteration, 0:groups - 1], shared_send.at[iteration])
        await_bytes(chosen.at[iteration, :, 0:rows - chunk, :], chosen_send.at[iteration])


def fused_device(groups, banks, log_density, assignment):
    members, cells = log_density.shape
    rows, chunk = G * members, G * members // banks
    width = PLANE // groups
    kept = G // banks * BARS
    line, pair = host_tables()
    tiled_pair = np.ascontiguousarray(pair.reshape(PLANE, groups, width).transpose(1, 0, 2))
    line_rows = np.kron(line, np.eye(members, dtype=np.float32))
    row_scale = (1.0 / line_rows.sum(axis=1, keepdims=True)).astype(np.float32)
    column_scale = (1.0 / pair.astype(np.float32).sum(axis=0, keepdims=True)).astype(np.float32)
    vmem = pl.BlockSpec(memory_space=pltpu.VMEM)
    dma = pltpu.SemaphoreType.DMA
    return pl.pallas_call(
        functools.partial(kernel, groups, banks, members),
        out_shape=(
            jax.ShapeDtypeStruct((BARS, cells // banks), BF16),
            jax.ShapeDtypeStruct((members, cells), F32),
        ),
        in_specs=[vmem, pl.BlockSpec(memory_space=pltpu.SMEM), pl.BlockSpec(memory_space=pl.ANY), vmem, vmem, vmem],
        out_specs=(vmem, vmem),
        scratch_shapes=[
            pltpu.VMEM((groups, PLANE, width), BF16),
            pltpu.VMEM((rows, PLANE), BF16),
            pltpu.VMEM((rows, PLANE), BF16),
            pltpu.VMEM((groups, rows, width), F32),
            pltpu.VMEM((groups, rows, width), F32),
            pltpu.VMEM((ITERS, groups, rows, width), BF16),
            pltpu.VMEM((ITERS, groups, rows, width), BF16),
            pltpu.VMEM((ITERS, groups, kept, width), F32),
            pltpu.VMEM((ITERS, groups, kept, width), F32),
            pltpu.VMEM((ITERS, groups, kept, width), BF16),
            pltpu.VMEM((ITERS, groups, rows, width), BF16),
            pltpu.VMEM((ITERS, groups, rows, width), BF16),
            pltpu.VMEM((rows, 128), BF16),
            pltpu.VMEM((chunk, 128), BF16),
            pltpu.VMEM((BARS, 128), F32),
            pltpu.VMEM((groups, BARS, 128), F32),
            dma, dma((2,)), dma((2,)),
            dma((ITERS,)), dma((ITERS, groups)),
            dma((ITERS, 2)),
            dma((ITERS,)), dma((ITERS, groups)),
            dma((ITERS,)), dma((ITERS, groups)),
        ],
        compiler_params=pltpu.CompilerParams(
            collective_id=0, has_side_effects=True, vmem_limit_bytes=40 * 1024 * 1024
        ),
    )(log_density, assignment, jnp.asarray(tiled_pair), jnp.asarray(line_rows), jnp.asarray(row_scale), jnp.asarray(column_scale))


def log_convolve(field_log, kernel_line, kernel_pair):
    member_count = field_log.shape[0]
    raised = jnp.exp(field_log).astype(BF16).reshape(member_count * G, PLANE)
    inner_sum = jnp.dot(raised, kernel_pair, preferred_element_type=F32).reshape(member_count, G, PLANE)
    outer_sum = jnp.einsum("ij,mjc->mic", kernel_line, inner_sum, precision=lax.Precision.HIGHEST)
    return jnp.log(outer_sum).reshape(member_count, G * PLANE)


def plain_device(log_density, assignment):
    line, pair = host_tables()
    kernel_line, kernel_pair = jnp.asarray(line), jnp.asarray(pair)
    member_count, cell_count = log_density.shape
    row_count = cell_count // 128
    labels = jnp.arange(BARS, dtype=jnp.int32)
    onehot = (assignment[:, None] == labels[None, :]).astype(F32)
    counts = lax.psum(jnp.sum(onehot, axis=0), ("blk", "bank"))
    potential = jnp.zeros((member_count, cell_count), F32)
    center_owned = None
    for _ in range(ITERS):
        source = log_density.astype(F32) - log_convolve(potential, kernel_line, kernel_pair)
        smoothed = log_convolve(source, kernel_line, kernel_pair)
        blocks = smoothed.reshape(member_count, row_count, 128)
        summed = jnp.einsum("mk,mrl->rkl", onehot, blocks, precision=lax.Precision.HIGHEST)
        summed = lax.psum_scatter(summed, "bank", scatter_dimension=0, tiled=True)
        summed = lax.psum(summed, "blk")
        center_owned = (summed / counts[None, :, None]).astype(BF16)
        center_all = lax.all_gather(center_owned, "bank", axis=0, tiled=True)
        chosen = jnp.einsum("mk,rkl->mrl", onehot.astype(BF16), center_all, preferred_element_type=F32)
        potential = chosen.reshape(member_count, cell_count) - smoothed
    centers = jnp.transpose(center_owned, (1, 0, 2)).reshape(BARS, center_owned.shape[0] * 128)
    return centers, potential


def solution(mesh):
    groups, banks = mesh.shape["blk"], mesh.shape["bank"]

    def per_device(log_density, assignment):
        rows = G * log_density.shape[0]
        fits = G % banks == 0 and (rows // banks) % 16 == 0 and PLANE % (128 * groups) == 0
        if fits and min(groups, banks) > 1:
            return fused_device(groups, banks, log_density, assignment)
        return plain_device(log_density, assignment)

    placed = (P(("blk", "bank"), None), P(("blk", "bank")))
    return jax.shard_map(
        per_device,
        mesh=mesh,
        in_specs=placed,
        out_specs=(P(None, "bank"), P(("blk", "bank"), None)),
        check_vma=False,
    )
```

```python
import functools

import jax
import jax.numpy as jnp
import ml_dtypes
import numpy as np
from jax import lax
from jax.experimental import pallas as pl
from jax.experimental.pallas import tpu as pltpu
from jax.sharding import PartitionSpec as P

G = 32
PLANE = G * G
BARS = 8
ITERS = 2
SENDS = 1
RETURNS = 1
MESH = pl.DeviceIdType.MESH
F32 = jnp.float32
BF16 = jnp.bfloat16


def host_tables():
    grid_pos = np.arange(G, dtype=np.float32)
    offset = grid_pos[:, None] - grid_pos[None, :]
    line = np.exp(np.float32(-0.5) * offset * offset)
    pair = (line[:, None, :, None] * line[None, :, None, :]).reshape(PLANE, PLANE).astype(ml_dtypes.bfloat16)
    return line, pair


def kernel(
    groups, banks, members,
    density_hbm, label_hbm, pair_hbm, line_hbm, scale_hbm,
    centers_ref, potential_ref,
    density_ref, label_ref, line_ref, scale_ref, pair, raised, source, lifted, smoothed, outgoing, incoming, partial, partial_in, shared, chosen, chosen_in,
    labels, label_out, count_out, count_in,
    load_sem, label_sem, count_sem, member_send, member_recv, partial_sem, shared_send, shared_recv, chosen_send, chosen_recv,
):
    blk, bank = lax.axis_index("blk"), lax.axis_index("bank")
    rows = G * members
    chunk = rows // banks
    slabs = G // banks
    width = PLANE // groups
    kept = slabs * BARS

    def group_at(step):
        return lax.rem(blk + step, groups)

    def bank_at(step):
        return lax.rem(bank + step, banks)

    def chunk_at(index):
        return pl.ds(pl.multiple_of(index * chunk, chunk), chunk)

    def part_at(step, parts):
        return lax.rem(blk // (groups // parts) + step, parts) * (groups // parts)

    def spread(src, dst, iteration, first, parts, send_sem, recv_sem):
        size = groups // parts
        for offset in range(size):
            dst[iteration, first + offset, chunk_at(bank), :] = src[iteration, first + offset, chunk_at(bank), :]
        for hop in range(1, banks):
            peer = bank_at(hop)
            push(
                src.at[iteration, pl.ds(first, size), chunk_at(peer), :],
                dst.at[iteration, pl.ds(first, size), chunk_at(bank), :],
                send_sem.at[iteration], recv_sem.at[iteration, first // size], (blk, peer),
            )

    def await_spread(dst, iteration, first, parts, recv_sem):
        size = groups // parts
        await_bytes(dst.at[iteration, pl.ds(first, size), 0:rows - chunk, :], recv_sem.at[iteration, first // size])

    def push(src, dst, send_sem, recv_sem, device):
        pltpu.make_async_remote_copy(
            src_ref=src, dst_ref=dst, send_sem=send_sem, recv_sem=recv_sem,
            device_id=device, device_id_type=MESH,
        ).start()

    def await_bytes(ref, sem):
        pltpu.make_async_copy(ref, ref, sem).wait()

    loads = [
        pltpu.make_async_copy(src, dst, load_sem.at[index])
        for index, (src, dst) in enumerate((
            (density_hbm, density_ref), (label_hbm, label_ref), (scale_hbm, scale_ref),
            (line_hbm, line_ref), (pair_hbm, pair),
        ))
    ]
    for load in loads:
        load.start()
    barrier = pltpu.get_barrier_semaphore()
    for step in range(1, banks):
        pl.semaphore_signal(barrier, inc=1, device_id=(blk, bank_at(step)), device_id_type=MESH)
    for step in range(1, groups):
        pl.semaphore_signal(barrier, inc=1, device_id=(group_at(step), bank), device_id_type=MESH)

    loads[1].wait()
    own_rows = lax.broadcasted_iota(jnp.int32, (chunk, 128), 0) % members
    own_labels = jnp.zeros((chunk, 128), F32)
    for member in range(members):
        own_labels = jnp.where(own_rows == member, label_ref[member].astype(F32), own_labels)
    label_out[...] = own_labels.astype(BF16)
    labels[chunk_at(bank), :] = own_labels.astype(BF16)

    loads[0].wait()
    for tile in range(groups):
        for x in range(G):
            lifted[tile, members * x:members * (x + 1), :] = density_ref[
                :, x * PLANE + tile * width:x * PLANE + (tile + 1) * width
            ].astype(F32)
    loads[2].wait()
    for tile in range(groups):
        risen = jnp.exp(lifted[tile])
        lifted[tile] = risen
        for part in range(width // 128):
            column = tile * (width // 128) + part
            scale = scale_ref[:rows, :] * scale_ref[rows + column:rows + column + 1, :]
            source[:, column * 128:(column + 1) * 128] = (risen[:, part * 128:(part + 1) * 128] * scale).astype(BF16)
    loads[3].wait()
    loads[4].wait()

    def convolve(field, tile):
        inner = jnp.dot(field, pair[tile], preferred_element_type=F32)
        high = inner.astype(BF16)
        low = (inner - high.astype(F32)).astype(BF16)
        return jnp.dot(line_ref[...], jnp.concatenate([high, high, low], axis=0), preferred_element_type=F32)

    pick = None
    for iteration in range(ITERS):
        last = iteration == ITERS - 1
        if iteration:
            for tile in range(groups):
                source[:, tile * width:(tile + 1) * width] = (lifted[tile] / convolve(raised[...], tile)).astype(BF16)

        for step in range(1, SENDS + 1):
            first = part_at(step, SENDS)
            for offset in range(groups // SENDS):
                tile = first + offset
                value = jnp.log(convolve(source[...], tile))
                smoothed[tile] = value
                outgoing[iteration, tile] = value.astype(BF16)
            if iteration == 0 and step == 1:
                pl.semaphore_wait(barrier, banks - 1 + groups - 1)
                for hop in range(1, banks):
                    push(label_out, labels.at[chunk_at(bank), :], label_sem.at[0], label_sem.at[1], (blk, bank_at(hop)))
            spread(outgoing, incoming, iteration, first, SENDS, member_send, member_recv)

        if iteration == 0:
            await_bytes(labels.at[0:rows - chunk, :], label_sem.at[1])
            row = lax.broadcasted_iota(jnp.int32, (rows, 128), 0)
            lane = lax.broadcasted_iota(jnp.int32, (rows, 128), 1)
            match = (labels[...].astype(F32) == (lane % BARS).astype(F32)) & ((row // members) % slabs == lane // BARS)
            pick_wide = jnp.where(match, 1.0, 0.0).astype(F32)
            gather_wide = jnp.transpose(pick_wide)
            pick = pick_wide.astype(BF16)[:, :kept]
            gather = gather_wide.astype(BF16)[:kept, :]
            own_count = jnp.broadcast_to(jnp.sum(gather_wide[:BARS, :], axis=1, keepdims=True), (BARS, 128))
            count_out[...] = own_count
            count_in[blk] = own_count
            for step in range(1, groups):
                push(count_out, count_in.at[blk], count_sem.at[0], count_sem.at[1], (group_at(step), bank))

        for step in range(1, SENDS + 1):
            first = part_at(step, SENDS)
            await_spread(incoming, iteration, first, SENDS, member_recv)
            for offset in range(groups // SENDS):
                tile = first + offset
                sums = jnp.dot(gather, incoming[iteration, tile], preferred_element_type=F32)
                partial[iteration, tile] = sums.astype(BF16)

                @pl.when(tile != blk)
                def _():
                    push(
                        partial.at[iteration, tile], partial_in.at[iteration, blk],
                        partial_sem.at[iteration, 0], partial_sem.at[iteration, 1], (tile, bank),
                    )
        partial_in[iteration, blk] = partial[iteration, blk]

        if iteration == 0:
            await_bytes(count_in.at[0:groups - 1], count_sem.at[1])
            counts = functools.reduce(jnp.add, [count_in[group] for group in range(groups)])
            counts = jnp.concatenate([counts[:, :1]] * slabs, axis=0)
        await_bytes(partial_in.at[iteration, 0:groups - 1], partial_sem.at[iteration, 1])
        total = functools.reduce(jnp.add, [partial_in[iteration, group].astype(F32) for group in range(groups)])
        shared[iteration, blk] = (total / counts).astype(BF16)
        for step in range(1, groups):
            push(
                shared.at[iteration, blk], shared.at[iteration, blk],
                shared_send.at[iteration], shared_recv.at[iteration, blk], (group_at(step), bank),
            )

        for step in range(RETURNS):
            first = part_at(step, RETURNS)
            for offset in range(groups // RETURNS):
                tile = first + offset

                @pl.when(tile != blk)
                def _():
                    await_bytes(shared.at[iteration, tile], shared_recv.at[iteration, tile])

                center = shared[iteration, tile]
                chosen[iteration, tile] = jnp.dot(pick, center, preferred_element_type=F32).astype(BF16)
            spread(chosen, chosen_in, iteration, first, RETURNS, chosen_send, chosen_recv)
            if last:
                for offset in range(groups // RETURNS):
                    tile = first + offset
                    for slab in range(slabs):
                        start = pl.multiple_of(slab * PLANE + tile * width, width)
                        centers_ref[:, pl.ds(start, width)] = shared[iteration, tile, slab * BARS:(slab + 1) * BARS, :]

        for step in range(RETURNS):
            first = part_at(step, RETURNS)
            await_spread(chosen_in, iteration, first, RETURNS, chosen_recv)
            for offset in range(groups // RETURNS):
                tile = first + offset
                value = chosen_in[iteration, tile].astype(F32) - smoothed[tile]
                if last:
                    for x in range(G):
                        start = pl.multiple_of(x * PLANE + tile * width, width)
                        potential_ref[:, pl.ds(start, width)] = value[members * x:members * (x + 1), :]
                else:
                    raised[:, pl.ds(pl.multiple_of(tile * width, width), width)] = jnp.exp(value).astype(BF16)

    for _ in range(banks - 1):
        await_bytes(label_out, label_sem.at[0])
    for _ in range(groups - 1):
        await_bytes(count_out, count_sem.at[0])
    for iteration in range(ITERS):
        await_bytes(outgoing.at[iteration, :, 0:rows - chunk, :], member_send.at[iteration])
        await_bytes(partial.at[iteration, 0:groups - 1], partial_sem.at[iteration, 0])
        await_bytes(shared.at[iteration, 0:groups - 1], shared_send.at[iteration])
        await_bytes(chosen.at[iteration, :, 0:rows - chunk, :], chosen_send.at[iteration])


def fused_device(groups, banks, log_density, assignment):
    members, cells = log_density.shape
    rows, chunk = G * members, G * members // banks
    width = PLANE // groups
    kept = G // banks * BARS
    line, pair = host_tables()
    tiled_pair = np.ascontiguousarray(pair.reshape(PLANE, groups, width).transpose(1, 0, 2))
    line_rows = np.kron(line, np.eye(members, dtype=np.float32))
    high = line_rows.astype(ml_dtypes.bfloat16)
    low = (line_rows - high.astype(np.float32)).astype(ml_dtypes.bfloat16)
    line_parts = np.concatenate([high, low, high], axis=1)
    row_scale = np.broadcast_to(1.0 / line_rows.sum(axis=1, keepdims=True), (rows, 128))
    column_scale = (1.0 / pair.astype(np.float32).sum(axis=0)).reshape(PLANE // 128, 128)
    scales = np.concatenate([row_scale, column_scale], axis=0).astype(np.float32)
    vmem = pl.BlockSpec(memory_space=pltpu.VMEM)
    dma = pltpu.SemaphoreType.DMA
    return pl.pallas_call(
        functools.partial(kernel, groups, banks, members),
        out_shape=(
            jax.ShapeDtypeStruct((BARS, cells // banks), BF16),
            jax.ShapeDtypeStruct((members, cells), F32),
        ),
        in_specs=[pl.BlockSpec(memory_space=pltpu.HBM)] * 5,
        out_specs=(vmem, vmem),
        scratch_shapes=[
            pltpu.VMEM(log_density.shape, BF16),
            pltpu.SMEM(assignment.shape, jnp.int32),
            pltpu.VMEM(line_parts.shape, BF16),
            pltpu.VMEM(scales.shape, F32),
            pltpu.VMEM((groups, PLANE, width), BF16),
            pltpu.VMEM((rows, PLANE), BF16),
            pltpu.VMEM((rows, PLANE), BF16),
            pltpu.VMEM((groups, rows, width), F32),
            pltpu.VMEM((groups, rows, width), F32),
            pltpu.VMEM((ITERS, groups, rows, width), BF16),
            pltpu.VMEM((ITERS, groups, rows, width), BF16),
            pltpu.VMEM((ITERS, groups, kept, width), BF16),
            pltpu.VMEM((ITERS, groups, kept, width), BF16),
            pltpu.VMEM((ITERS, groups, kept, width), BF16),
            pltpu.VMEM((ITERS, groups, rows, width), BF16),
            pltpu.VMEM((ITERS, groups, rows, width), BF16),
            pltpu.VMEM((rows, 128), BF16),
            pltpu.VMEM((chunk, 128), BF16),
            pltpu.VMEM((BARS, 128), F32),
            pltpu.VMEM((groups, BARS, 128), F32),
            dma((5,)), dma((2,)), dma((2,)),
            dma((ITERS,)), dma((ITERS, groups)),
            dma((ITERS, 2)),
            dma((ITERS,)), dma((ITERS, groups)),
            dma((ITERS,)), dma((ITERS, groups)),
        ],
        compiler_params=pltpu.CompilerParams(
            collective_id=0, has_side_effects=True, vmem_limit_bytes=64 * 1024 * 1024 - 640 * 1024
        ),
    )(log_density, assignment, jnp.asarray(tiled_pair), jnp.asarray(line_parts), jnp.asarray(scales))


def log_convolve(field_log, kernel_line, kernel_pair):
    member_count = field_log.shape[0]
    raised = jnp.exp(field_log).astype(BF16).reshape(member_count * G, PLANE)
    inner_sum = jnp.dot(raised, kernel_pair, preferred_element_type=F32).reshape(member_count, G, PLANE)
    outer_sum = jnp.einsum("ij,mjc->mic", kernel_line, inner_sum, precision=lax.Precision.HIGHEST)
    return jnp.log(outer_sum).reshape(member_count, G * PLANE)


def plain_device(log_density, assignment):
    line, pair = host_tables()
    kernel_line, kernel_pair = jnp.asarray(line), jnp.asarray(pair)
    member_count, cell_count = log_density.shape
    row_count = cell_count // 128
    labels = jnp.arange(BARS, dtype=jnp.int32)
    onehot = (assignment[:, None] == labels[None, :]).astype(F32)
    counts = lax.psum(jnp.sum(onehot, axis=0), ("blk", "bank"))
    potential = jnp.zeros((member_count, cell_count), F32)
    center_owned = None
    for _ in range(ITERS):
        source = log_density.astype(F32) - log_convolve(potential, kernel_line, kernel_pair)
        smoothed = log_convolve(source, kernel_line, kernel_pair)
        blocks = smoothed.reshape(member_count, row_count, 128)
        summed = jnp.einsum("mk,mrl->rkl", onehot, blocks, precision=lax.Precision.HIGHEST)
        summed = lax.psum_scatter(summed, "bank", scatter_dimension=0, tiled=True)
        summed = lax.psum(summed, "blk")
        center_owned = (summed / counts[None, :, None]).astype(BF16)
        center_all = lax.all_gather(center_owned, "bank", axis=0, tiled=True)
        chosen = jnp.einsum("mk,rkl->mrl", onehot.astype(BF16), center_all, preferred_element_type=F32)
        potential = chosen.reshape(member_count, cell_count) - smoothed
    centers = jnp.transpose(center_owned, (1, 0, 2)).reshape(BARS, center_owned.shape[0] * 128)
    return centers, potential


def solution(mesh):
    groups, banks = mesh.shape["blk"], mesh.shape["bank"]

    def per_device(log_density, assignment):
        rows = G * log_density.shape[0]
        fits = G % banks == 0 and (rows // banks) % 16 == 0 and PLANE % (128 * groups) == 0
        if fits and min(groups, banks) > 1:
            return fused_device(groups, banks, log_density, assignment)
        return plain_device(log_density, assignment)

    placed = (P(("blk", "bank"), None), P(("blk", "bank")))
    return jax.shard_map(
        per_device,
        mesh=mesh,
        in_specs=placed,
        out_specs=(P(None, "bank"), P(("blk", "bank"), None)),
        check_vma=False,
    )
```

```python
import functools

import jax
import jax.numpy as jnp
import ml_dtypes
import numpy as np
from jax import lax
from jax.experimental import pallas as pl
from jax.experimental.pallas import tpu as pltpu
from jax.sharding import PartitionSpec as P

G = 32
PLANE = G * G
BARS = 8
ITERS = 2
MESH = pl.DeviceIdType.MESH
F32 = jnp.float32
BF16 = jnp.bfloat16


def host_tables():
    grid_pos = np.arange(G, dtype=np.float32)
    offset = grid_pos[:, None] - grid_pos[None, :]
    line = np.exp(np.float32(-0.5) * offset * offset)
    pair = (line[:, None, :, None] * line[None, :, None, :]).reshape(PLANE, PLANE).astype(ml_dtypes.bfloat16)
    return line, pair


def kernel(
    groups, banks, members,
    density_hbm, label_hbm, pair_hbm, line_hbm, scale_hbm,
    centers_ref, potential_ref,
    density_ref, label_ref, line_ref, scale_ref, pair, raised, source, lifted, smoothed, outgoing, incoming, partial, partial_in, shared, chosen, chosen_in,
    labels, label_out, count_out, count_in,
    load_sem, label_sem, count_sem, member_send, member_recv, partial_sem, shared_send, shared_recv, chosen_send, chosen_recv,
):
    blk, bank = lax.axis_index("blk"), lax.axis_index("bank")
    rows = G * members
    chunk = rows // banks
    slabs = G // banks
    width = PLANE // groups
    kept = slabs * BARS

    def group_at(step):
        return lax.rem(blk + step, groups)

    def bank_at(step):
        return lax.rem(bank + step, banks)

    def chunk_at(index):
        return pl.ds(pl.multiple_of(index * chunk, chunk), chunk)

    def tile_at(step):
        if step == groups - 1:
            return blk
        up = step + (blk <= step).astype(jnp.int32)
        down = groups - 1 - step - (groups - 1 - blk <= step).astype(jnp.int32)
        return jnp.where(2 * blk >= groups, up, down)

    def spread(src, dst, iteration, tile, send_sem, recv_sem):
        for hop in range(1, banks):
            peer = bank_at(hop)
            push(
                src.at[iteration, tile, chunk_at(peer), :], dst.at[iteration, tile, chunk_at(bank), :],
                send_sem.at[iteration], recv_sem.at[iteration, tile], (blk, peer),
            )
        dst[iteration, tile, chunk_at(bank), :] = src[iteration, tile, chunk_at(bank), :]

    def await_spread(dst, iteration, tile, recv_sem):
        await_bytes(dst.at[iteration, tile, 0:rows - chunk, :], recv_sem.at[iteration, tile])

    def push(src, dst, send_sem, recv_sem, device):
        pltpu.make_async_remote_copy(
            src_ref=src, dst_ref=dst, send_sem=send_sem, recv_sem=recv_sem,
            device_id=device, device_id_type=MESH,
        ).start()

    def await_bytes(ref, sem):
        pltpu.make_async_copy(ref, ref, sem).wait()

    loads = [
        pltpu.make_async_copy(src, dst, load_sem.at[index])
        for index, (src, dst) in enumerate((
            (density_hbm, density_ref), (label_hbm, label_ref), (scale_hbm, scale_ref),
            (line_hbm, line_ref), (pair_hbm, pair),
        ))
    ]
    for load in loads:
        load.start()
    barrier = pltpu.get_barrier_semaphore()
    for step in range(1, banks):
        pl.semaphore_signal(barrier, inc=1, device_id=(blk, bank_at(step)), device_id_type=MESH)
    for step in range(1, groups):
        pl.semaphore_signal(barrier, inc=1, device_id=(group_at(step), bank), device_id_type=MESH)

    loads[1].wait()
    own_rows = lax.broadcasted_iota(jnp.int32, (chunk, 128), 0) % members
    own_labels = jnp.zeros((chunk, 128), F32)
    for member in range(members):
        own_labels = jnp.where(own_rows == member, label_ref[member].astype(F32), own_labels)
    label_out[...] = own_labels.astype(BF16)
    labels[chunk_at(bank), :] = own_labels.astype(BF16)

    loads[0].wait()
    for tile in range(groups):
        for x in range(G):
            lifted[tile, members * x:members * (x + 1), :] = density_ref[
                :, x * PLANE + tile * width:x * PLANE + (tile + 1) * width
            ].astype(F32)
    loads[2].wait()
    for tile in range(groups):
        risen = jnp.exp(lifted[tile])
        lifted[tile] = risen
        for part in range(width // 128):
            column = tile * (width // 128) + part
            scale = scale_ref[:rows, :] * scale_ref[rows + column:rows + column + 1, :]
            source[:, column * 128:(column + 1) * 128] = (risen[:, part * 128:(part + 1) * 128] * scale).astype(BF16)
    loads[3].wait()
    loads[4].wait()

    def convolve(field, tile):
        inner = jnp.dot(field, pair[tile], preferred_element_type=F32)
        high = inner.astype(BF16)
        low = (inner - high.astype(F32)).astype(BF16)
        return jnp.dot(line_ref[...], jnp.concatenate([high, high, low], axis=0), preferred_element_type=F32)

    pick = None
    for iteration in range(ITERS):
        last = iteration == ITERS - 1
        if iteration:
            for tile in range(groups):
                source[:, tile * width:(tile + 1) * width] = (lifted[tile] / convolve(raised[...], tile)).astype(BF16)

        for step in range(groups):
            tile = tile_at(step)
            value = jnp.log(convolve(source[...], tile))
            smoothed[tile] = value
            outgoing[iteration, tile] = value.astype(BF16)
            if iteration == 0 and step == 0:
                pl.semaphore_wait(barrier, banks - 1 + groups - 1)
                for hop in range(1, banks):
                    push(label_out, labels.at[chunk_at(bank), :], label_sem.at[0], label_sem.at[1], (blk, bank_at(hop)))
            spread(outgoing, incoming, iteration, tile, member_send, member_recv)

        if iteration == 0:
            await_bytes(labels.at[0:rows - chunk, :], label_sem.at[1])
            row = lax.broadcasted_iota(jnp.int32, (rows, 128), 0)
            lane = lax.broadcasted_iota(jnp.int32, (rows, 128), 1)
            match = (labels[...].astype(F32) == (lane % BARS).astype(F32)) & ((row // members) % slabs == lane // BARS)
            pick_wide = jnp.where(match, 1.0, 0.0).astype(F32)
            gather_wide = jnp.transpose(pick_wide)
            pick = pick_wide.astype(BF16)[:, :kept]
            gather = gather_wide.astype(BF16)[:kept, :]
            own_count = jnp.broadcast_to(jnp.sum(gather_wide[:BARS, :], axis=1, keepdims=True), (BARS, 128))
            count_out[...] = own_count
            count_in[blk] = own_count
            for step in range(1, groups):
                push(count_out, count_in.at[blk], count_sem.at[0], count_sem.at[1], (group_at(step), bank))

        for step in range(groups):
            tile = tile_at(step)
            await_spread(incoming, iteration, tile, member_recv)
            sums = jnp.dot(gather, incoming[iteration, tile], preferred_element_type=F32)
            if step < groups - 1:
                partial[iteration, tile] = sums
                push(
                    partial.at[iteration, tile], partial_in.at[iteration, blk],
                    partial_sem.at[iteration, 0], partial_sem.at[iteration, 1], (tile, bank),
                )
            else:
                partial_in[iteration, blk] = sums

        if iteration == 0:
            await_bytes(count_in.at[0:groups - 1], count_sem.at[1])
            counts = functools.reduce(jnp.add, [count_in[group] for group in range(groups)])
            counts = jnp.concatenate([counts[:, :1]] * slabs, axis=0)
        await_bytes(partial_in.at[iteration, 0:groups - 1], partial_sem.at[iteration, 1])
        total = functools.reduce(jnp.add, [partial_in[iteration, group] for group in range(groups)])
        shared[iteration, blk] = (total / counts).astype(BF16)
        for step in range(groups - 1):
            push(
                shared.at[iteration, blk], shared.at[iteration, blk],
                shared_send.at[iteration], shared_recv.at[iteration, blk], (tile_at(step), bank),
            )

        for step in reversed(range(groups)):
            tile = tile_at(step)
            if step < groups - 1:
                await_bytes(shared.at[iteration, tile], shared_recv.at[iteration, tile])
            center = shared[iteration, tile]
            chosen[iteration, tile] = jnp.dot(pick, center, preferred_element_type=F32).astype(BF16)
            spread(chosen, chosen_in, iteration, tile, chosen_send, chosen_recv)
            if last:
                for slab in range(slabs):
                    start = pl.multiple_of(slab * PLANE + tile * width, width)
                    centers_ref[:, pl.ds(start, width)] = center[slab * BARS:(slab + 1) * BARS, :]

        for step in reversed(range(groups)):
            tile = tile_at(step)
            await_spread(chosen_in, iteration, tile, chosen_recv)
            value = chosen_in[iteration, tile].astype(F32) - smoothed[tile]
            if last:
                for x in range(G):
                    start = pl.multiple_of(x * PLANE + tile * width, width)
                    potential_ref[:, pl.ds(start, width)] = value[members * x:members * (x + 1), :]
            else:
                raised[:, pl.ds(pl.multiple_of(tile * width, width), width)] = jnp.exp(value).astype(BF16)

    for _ in range(banks - 1):
        await_bytes(label_out, label_sem.at[0])
    for _ in range(groups - 1):
        await_bytes(count_out, count_sem.at[0])
    for iteration in range(ITERS):
        await_bytes(outgoing.at[iteration, :, 0:rows - chunk, :], member_send.at[iteration])
        await_bytes(partial.at[iteration, 0:groups - 1], partial_sem.at[iteration, 0])
        await_bytes(shared.at[iteration, 0:groups - 1], shared_send.at[iteration])
        await_bytes(chosen.at[iteration, :, 0:rows - chunk, :], chosen_send.at[iteration])


def fused_device(groups, banks, log_density, assignment):
    members, cells = log_density.shape
    rows, chunk = G * members, G * members // banks
    width = PLANE // groups
    kept = G // banks * BARS
    line, pair = host_tables()
    tiled_pair = np.ascontiguousarray(pair.reshape(PLANE, groups, width).transpose(1, 0, 2))
    line_rows = np.kron(line, np.eye(members, dtype=np.float32))
    high = line_rows.astype(ml_dtypes.bfloat16)
    low = (line_rows - high.astype(np.float32)).astype(ml_dtypes.bfloat16)
    line_parts = np.concatenate([high, low, high], axis=1)
    row_scale = np.broadcast_to(1.0 / line_rows.sum(axis=1, keepdims=True), (rows, 128))
    column_scale = (1.0 / pair.astype(np.float32).sum(axis=0)).reshape(PLANE // 128, 128)
    scales = np.concatenate([row_scale, column_scale], axis=0).astype(np.float32)
    operands = (log_density, assignment, jnp.asarray(tiled_pair), jnp.asarray(line_parts), jnp.asarray(scales))
    vmem = pl.BlockSpec(memory_space=pltpu.VMEM)
    dma = pltpu.SemaphoreType.DMA
    return pl.pallas_call(
        functools.partial(kernel, groups, banks, members),
        out_shape=(
            jax.ShapeDtypeStruct((BARS, cells // banks), BF16),
            jax.ShapeDtypeStruct((members, cells), F32),
        ),
        in_specs=[pl.BlockSpec(memory_space=pltpu.HBM)] * 5,
        out_specs=(vmem, vmem),
        scratch_shapes=[
            pltpu.VMEM(log_density.shape, BF16),
            pltpu.SMEM(assignment.shape, jnp.int32),
            pltpu.VMEM(line_parts.shape, BF16),
            pltpu.VMEM(scales.shape, F32),
            pltpu.VMEM((groups, PLANE, width), BF16),
            pltpu.VMEM((rows, PLANE), BF16),
            pltpu.VMEM((rows, PLANE), BF16),
            pltpu.VMEM((groups, rows, width), F32),
            pltpu.VMEM((groups, rows, width), F32),
            pltpu.VMEM((ITERS, groups, rows, width), BF16),
            pltpu.VMEM((ITERS, groups, rows, width), BF16),
            pltpu.VMEM((ITERS, groups, kept, width), F32),
            pltpu.VMEM((ITERS, groups, kept, width), F32),
            pltpu.VMEM((ITERS, groups, kept, width), BF16),
            pltpu.VMEM((ITERS, groups, rows, width), BF16),
            pltpu.VMEM((ITERS, groups, rows, width), BF16),
            pltpu.VMEM((rows, 128), BF16),
            pltpu.VMEM((chunk, 128), BF16),
            pltpu.VMEM((BARS, 128), F32),
            pltpu.VMEM((groups, BARS, 128), F32),
            dma((5,)), dma((2,)), dma((2,)),
            dma((ITERS,)), dma((ITERS, groups)),
            dma((ITERS, 2)),
            dma((ITERS,)), dma((ITERS, groups)),
            dma((ITERS,)), dma((ITERS, groups)),
        ],
        compiler_params=pltpu.CompilerParams(
            collective_id=0, has_side_effects=True, vmem_limit_bytes=40 * 1024 * 1024
        ),
    )(*(pltpu.with_memory_space_constraint(operand, pltpu.HBM) for operand in operands))


def log_convolve(field_log, kernel_line, kernel_pair):
    member_count = field_log.shape[0]
    raised = jnp.exp(field_log).astype(BF16).reshape(member_count * G, PLANE)
    inner_sum = jnp.dot(raised, kernel_pair, preferred_element_type=F32).reshape(member_count, G, PLANE)
    outer_sum = jnp.einsum("ij,mjc->mic", kernel_line, inner_sum, precision=lax.Precision.HIGHEST)
    return jnp.log(outer_sum).reshape(member_count, G * PLANE)


def plain_device(log_density, assignment):
    line, pair = host_tables()
    kernel_line, kernel_pair = jnp.asarray(line), jnp.asarray(pair)
    member_count, cell_count = log_density.shape
    row_count = cell_count // 128
    labels = jnp.arange(BARS, dtype=jnp.int32)
    onehot = (assignment[:, None] == labels[None, :]).astype(F32)
    counts = lax.psum(jnp.sum(onehot, axis=0), ("blk", "bank"))
    potential = jnp.zeros((member_count, cell_count), F32)
    center_owned = None
    for _ in range(ITERS):
        source = log_density.astype(F32) - log_convolve(potential, kernel_line, kernel_pair)
        smoothed = log_convolve(source, kernel_line, kernel_pair)
        blocks = smoothed.reshape(member_count, row_count, 128)
        summed = jnp.einsum("mk,mrl->rkl", onehot, blocks, precision=lax.Precision.HIGHEST)
        summed = lax.psum_scatter(summed, "bank", scatter_dimension=0, tiled=True)
        summed = lax.psum(summed, "blk")
        center_owned = (summed / counts[None, :, None]).astype(BF16)
        center_all = lax.all_gather(center_owned, "bank", axis=0, tiled=True)
        chosen = jnp.einsum("mk,rkl->mrl", onehot.astype(BF16), center_all, preferred_element_type=F32)
        potential = chosen.reshape(member_count, cell_count) - smoothed
    centers = jnp.transpose(center_owned, (1, 0, 2)).reshape(BARS, center_owned.shape[0] * 128)
    return centers, potential


def solution(mesh):
    groups, banks = mesh.shape["blk"], mesh.shape["bank"]

    def per_device(log_density, assignment):
        rows = G * log_density.shape[0]
        fits = G % banks == 0 and (rows // banks) % 16 == 0 and PLANE % (128 * groups) == 0
        if fits and min(groups, banks) > 1:
            return fused_device(groups, banks, log_density, assignment)
        return plain_device(log_density, assignment)

    placed = (P(("blk", "bank"), None), P(("blk", "bank")))
    return jax.shard_map(
        per_device,
        mesh=mesh,
        in_specs=placed,
        out_specs=(P(None, "bank"), P(("blk", "bank"), None)),
        check_vma=False,
    )
```

```python
import functools

import jax
import jax.numpy as jnp
import ml_dtypes
import numpy as np
from jax import lax
from jax.experimental import pallas as pl
from jax.experimental.pallas import tpu as pltpu
from jax.sharding import PartitionSpec as P

G = 32
PLANE = G * G
BARS = 8
ITERS = 2
MESH = pl.DeviceIdType.MESH
F32 = jnp.float32
BF16 = jnp.bfloat16


def host_tables():
    grid_pos = np.arange(G, dtype=np.float32)
    offset = grid_pos[:, None] - grid_pos[None, :]
    line = np.exp(np.float32(-0.5) * offset * offset)
    pair = (line[:, None, :, None] * line[None, :, None, :]).reshape(PLANE, PLANE).astype(ml_dtypes.bfloat16)
    return line, pair


def kernel(
    groups, banks, members,
    density_hbm, label_hbm, pair_hbm, line_hbm, scale_hbm,
    centers_ref, potential_ref,
    density_ref, label_ref, line_ref, scale_ref, pair, source, running, lifted, smoothed, outgoing, incoming, partial, partial_in, shared, chosen, chosen_in,
    labels, label_out, count_out, count_in,
    load_sem, label_sem, count_sem, member_send, member_recv, partial_sem, shared_send, shared_recv, chosen_send, chosen_recv,
):
    blk, bank = lax.axis_index("blk"), lax.axis_index("bank")
    rows = G * members
    chunk = rows // banks
    slabs = G // banks
    width = PLANE // groups
    kept = slabs * BARS

    def group_at(step):
        return lax.rem(blk + step, groups)

    def bank_at(step):
        return lax.rem(bank + step, banks)

    def chunk_at(index):
        return pl.ds(pl.multiple_of(index * chunk, chunk), chunk)

    def tile_at(step):
        if step == groups - 1:
            return blk
        up = step + (blk <= step).astype(jnp.int32)
        down = groups - 1 - step - (groups - 1 - blk <= step).astype(jnp.int32)
        return jnp.where(2 * blk >= groups, up, down)

    def spread(src, dst, iteration, tile, send_sem, recv_sem):
        for hop in range(1, banks):
            peer = bank_at(hop)
            push(
                src.at[iteration, tile, chunk_at(peer), :], dst.at[iteration, tile, chunk_at(bank), :],
                send_sem.at[iteration], recv_sem.at[iteration, tile], (blk, peer),
            )
        dst[iteration, tile, chunk_at(bank), :] = src[iteration, tile, chunk_at(bank), :]

    def await_spread(dst, iteration, tile, recv_sem):
        await_bytes(dst.at[iteration, tile, 0:rows - chunk, :], recv_sem.at[iteration, tile])

    def push(src, dst, send_sem, recv_sem, device):
        pltpu.make_async_remote_copy(
            src_ref=src, dst_ref=dst, send_sem=send_sem, recv_sem=recv_sem,
            device_id=device, device_id_type=MESH,
        ).start()

    def await_bytes(ref, sem):
        pltpu.make_async_copy(ref, ref, sem).wait()

    loads = [
        pltpu.make_async_copy(src, dst, load_sem.at[index])
        for index, (src, dst) in enumerate((
            (density_hbm, density_ref), (label_hbm, label_ref), (scale_hbm, scale_ref), (line_hbm, line_ref),
        ))
    ]
    for step in range(groups):
        tile = tile_at(step)
        loads.append(pltpu.make_async_copy(pair_hbm.at[tile], pair.at[tile], load_sem.at[4 + step]))
    for load in loads:
        load.start()
    barrier = pltpu.get_barrier_semaphore()
    for step in range(1, banks):
        pl.semaphore_signal(barrier, inc=1, device_id=(blk, bank_at(step)), device_id_type=MESH)
    for step in range(1, groups):
        pl.semaphore_signal(barrier, inc=1, device_id=(group_at(step), bank), device_id_type=MESH)

    loads[1].wait()
    own_rows = lax.broadcasted_iota(jnp.int32, (chunk, 128), 0) % members
    own_labels = jnp.zeros((chunk, 128), F32)
    for member in range(members):
        own_labels = jnp.where(own_rows == member, label_ref[member].astype(F32), own_labels)
    label_out[...] = own_labels.astype(BF16)
    labels[chunk_at(bank), :] = own_labels.astype(BF16)

    loads[0].wait()
    for tile in range(groups):
        for x in range(G):
            lifted[tile, members * x:members * (x + 1), :] = density_ref[
                :, x * PLANE + tile * width:x * PLANE + (tile + 1) * width
            ].astype(F32)
    loads[2].wait()
    for tile in range(groups):
        risen = jnp.exp(lifted[tile])
        lifted[tile] = risen
        for part in range(width // 128):
            column = tile * (width // 128) + part
            scale = scale_ref[:rows, :] * scale_ref[rows + column:rows + column + 1, :]
            source[:, column * 128:(column + 1) * 128] = (risen[:, part * 128:(part + 1) * 128] * scale).astype(BF16)
    loads[3].wait()

    def across(inner):
        high = inner.astype(BF16)
        low = (inner - high.astype(F32)).astype(BF16)
        return jnp.dot(line_ref[...], jnp.concatenate([high, high, low], axis=0), preferred_element_type=F32)

    pick = None
    for iteration in range(ITERS):
        last = iteration == ITERS - 1
        for step in range(groups):
            tile = tile_at(step)
            if iteration == 0:
                loads[4 + step].wait()
            value = jnp.log(across(jnp.dot(source[...], pair[tile], preferred_element_type=F32)))
            smoothed[tile] = value
            outgoing[iteration, tile] = value.astype(BF16)
            if iteration == 0 and step == 0:
                pl.semaphore_wait(barrier, banks - 1 + groups - 1)
            spread(outgoing, incoming, iteration, tile, member_send, member_recv)
            if iteration == 0 and step == 0:
                for hop in range(1, banks):
                    push(label_out, labels.at[chunk_at(bank), :], label_sem.at[0], label_sem.at[1], (blk, bank_at(hop)))

        if iteration == 0:
            await_bytes(labels.at[0:rows - chunk, :], label_sem.at[1])
            row = lax.broadcasted_iota(jnp.int32, (rows, 128), 0)
            lane = lax.broadcasted_iota(jnp.int32, (rows, 128), 1)
            match = (labels[...].astype(F32) == (lane % BARS).astype(F32)) & ((row // members) % slabs == lane // BARS)
            pick_wide = jnp.where(match, 1.0, 0.0).astype(F32)
            gather_wide = jnp.transpose(pick_wide)
            pick = pick_wide.astype(BF16)[:, :kept]
            gather = gather_wide.astype(BF16)[:kept, :]
            own_count = jnp.broadcast_to(jnp.sum(gather_wide[:BARS, :], axis=1, keepdims=True), (BARS, 128))
            count_out[...] = own_count
            count_in[blk] = own_count
            for step in range(1, groups):
                push(count_out, count_in.at[blk], count_sem.at[0], count_sem.at[1], (group_at(step), bank))

        for step in range(groups):
            tile = tile_at(step)
            await_spread(incoming, iteration, tile, member_recv)
            sums = jnp.dot(gather, incoming[iteration, tile], preferred_element_type=F32)
            if step < groups - 1:
                partial[iteration, tile] = sums
                push(
                    partial.at[iteration, tile], partial_in.at[iteration, blk],
                    partial_sem.at[iteration, 0], partial_sem.at[iteration, 1], (tile, bank),
                )
            else:
                partial_in[iteration, blk] = sums

        if iteration == 0:
            await_bytes(count_in.at[0:groups - 1], count_sem.at[1])
            counts = functools.reduce(jnp.add, [count_in[group] for group in range(groups)])
            counts = jnp.concatenate([counts[:, :1]] * slabs, axis=0)
        await_bytes(partial_in.at[iteration, 0:groups - 1], partial_sem.at[iteration, 1])
        total = functools.reduce(jnp.add, [partial_in[iteration, group] for group in range(groups)])
        shared[iteration, blk] = (total / counts).astype(BF16)
        for step in range(groups - 1):
            push(
                shared.at[iteration, blk], shared.at[iteration, blk],
                shared_send.at[iteration], shared_recv.at[iteration, blk], (tile_at(step), bank),
            )

        for step in reversed(range(groups)):
            tile = tile_at(step)
            if step < groups - 1:
                await_bytes(shared.at[iteration, tile], shared_recv.at[iteration, tile])
            center = shared[iteration, tile]
            chosen[iteration, tile] = jnp.dot(pick, center, preferred_element_type=F32).astype(BF16)
            spread(chosen, chosen_in, iteration, tile, chosen_send, chosen_recv)
            if last:
                for slab in range(slabs):
                    start = pl.multiple_of(slab * PLANE + tile * width, width)
                    centers_ref[:, pl.ds(start, width)] = center[slab * BARS:(slab + 1) * BARS, :]

        for step in reversed(range(groups)):
            tile = tile_at(step)
            await_spread(chosen_in, iteration, tile, chosen_recv)
            value = chosen_in[iteration, tile].astype(F32) - smoothed[tile]
            if last:
                for x in range(G):
                    start = pl.multiple_of(x * PLANE + tile * width, width)
                    potential_ref[:, pl.ds(start, width)] = value[members * x:members * (x + 1), :]
            else:
                raised = jnp.exp(value).astype(BF16)
                depth = pl.ds(pl.multiple_of(tile * width, width), width)
                for target in range(groups):
                    inner = jnp.dot(raised, pair[target, depth, :], preferred_element_type=F32)
                    if step < groups - 1:
                        inner += running[target]
                    if step:
                        running[target] = inner
                    else:
                        columns = slice(target * width, (target + 1) * width)
                        source[:, columns] = (lifted[target] / across(inner)).astype(BF16)

    for _ in range(banks - 1):
        await_bytes(label_out, label_sem.at[0])
    for _ in range(groups - 1):
        await_bytes(count_out, count_sem.at[0])
    for iteration in range(ITERS):
        await_bytes(outgoing.at[iteration, :, 0:rows - chunk, :], member_send.at[iteration])
        await_bytes(partial.at[iteration, 0:groups - 1], partial_sem.at[iteration, 0])
        await_bytes(shared.at[iteration, 0:groups - 1], shared_send.at[iteration])
        await_bytes(chosen.at[iteration, :, 0:rows - chunk, :], chosen_send.at[iteration])


def store_results(centers_in, potential_in, centers_out, potential_out, sems):
    copies = [
        pltpu.make_async_copy(centers_in, centers_out, sems.at[0]),
        pltpu.make_async_copy(potential_in, potential_out, sems.at[1]),
    ]
    for copy in copies:
        copy.start()
    for copy in copies:
        copy.wait()


def fused_device(groups, banks, log_density, assignment):
    members, cells = log_density.shape
    rows, chunk = G * members, G * members // banks
    width = PLANE // groups
    kept = G // banks * BARS
    line, pair = host_tables()
    tiled_pair = np.ascontiguousarray(pair.reshape(PLANE, groups, width).transpose(1, 0, 2))
    line_rows = np.kron(line, np.eye(members, dtype=np.float32))
    high = line_rows.astype(ml_dtypes.bfloat16)
    low = (line_rows - high.astype(np.float32)).astype(ml_dtypes.bfloat16)
    line_parts = np.concatenate([high, low, high], axis=1)
    row_scale = np.broadcast_to(1.0 / line_rows.sum(axis=1, keepdims=True), (rows, 128))
    column_scale = (1.0 / pair.astype(np.float32).sum(axis=0)).reshape(PLANE // 128, 128)
    scales = np.concatenate([row_scale, column_scale], axis=0).astype(np.float32)
    operands = (log_density, assignment, jnp.asarray(tiled_pair), jnp.asarray(line_parts), jnp.asarray(scales))
    vmem = pl.BlockSpec(memory_space=pltpu.VMEM)
    dma = pltpu.SemaphoreType.DMA
    results = pl.pallas_call(
        functools.partial(kernel, groups, banks, members),
        out_shape=(
            jax.ShapeDtypeStruct((BARS, cells // banks), BF16),
            jax.ShapeDtypeStruct((members, cells), F32),
        ),
        in_specs=[pl.BlockSpec(memory_space=pltpu.HBM)] * 5,
        out_specs=(vmem, vmem),
        scratch_shapes=[
            pltpu.VMEM(log_density.shape, BF16),
            pltpu.SMEM(assignment.shape, jnp.int32),
            pltpu.VMEM(line_parts.shape, BF16),
            pltpu.VMEM(scales.shape, F32),
            pltpu.VMEM((groups, PLANE, width), BF16),
            pltpu.VMEM((rows, PLANE), BF16),
            pltpu.VMEM((groups, rows, width), F32),
            pltpu.VMEM((groups, rows, width), F32),
            pltpu.VMEM((groups, rows, width), F32),
            pltpu.VMEM((ITERS, groups, rows, width), BF16),
            pltpu.VMEM((ITERS, groups, rows, width), BF16),
            pltpu.VMEM((ITERS, groups, kept, width), F32),
            pltpu.VMEM((ITERS, groups, kept, width), F32),
            pltpu.VMEM((ITERS, groups, kept, width), BF16),
            pltpu.VMEM((ITERS, groups, rows, width), BF16),
            pltpu.VMEM((ITERS, groups, rows, width), BF16),
            pltpu.VMEM((rows, 128), BF16),
            pltpu.VMEM((chunk, 128), BF16),
            pltpu.VMEM((BARS, 128), F32),
            pltpu.VMEM((groups, BARS, 128), F32),
            dma((4 + groups,)), dma((2,)), dma((2,)),
            dma((ITERS,)), dma((ITERS, groups)),
            dma((ITERS, 2)),
            dma((ITERS,)), dma((ITERS, groups)),
            dma((ITERS,)), dma((ITERS, groups)),
        ],
        compiler_params=pltpu.CompilerParams(
            collective_id=0, has_side_effects=True, vmem_limit_bytes=40 * 1024 * 1024
        ),
    )(*(pltpu.with_memory_space_constraint(operand, pltpu.HBM) for operand in operands))
    return pl.pallas_call(
        store_results,
        out_shape=tuple(jax.ShapeDtypeStruct(result.shape, result.dtype) for result in results),
        in_specs=[pl.BlockSpec(memory_space=pl.ANY)] * 2,
        out_specs=(pl.BlockSpec(memory_space=pl.ANY),) * 2,
        scratch_shapes=[dma((2,))],
    )(*results)


def log_convolve(field_log, kernel_line, kernel_pair):
    member_count = field_log.shape[0]
    raised = jnp.exp(field_log).astype(BF16).reshape(member_count * G, PLANE)
    inner_sum = jnp.dot(raised, kernel_pair, preferred_element_type=F32).reshape(member_count, G, PLANE)
    outer_sum = jnp.einsum("ij,mjc->mic", kernel_line, inner_sum, precision=lax.Precision.HIGHEST)
    return jnp.log(outer_sum).reshape(member_count, G * PLANE)


def plain_device(log_density, assignment):
    line, pair = host_tables()
    kernel_line, kernel_pair = jnp.asarray(line), jnp.asarray(pair)
    member_count, cell_count = log_density.shape
    row_count = cell_count // 128
    labels = jnp.arange(BARS, dtype=jnp.int32)
    onehot = (assignment[:, None] == labels[None, :]).astype(F32)
    counts = lax.psum(jnp.sum(onehot, axis=0), ("blk", "bank"))
    potential = jnp.zeros((member_count, cell_count), F32)
    center_owned = None
    for _ in range(ITERS):
        source = log_density.astype(F32) - log_convolve(potential, kernel_line, kernel_pair)
        smoothed = log_convolve(source, kernel_line, kernel_pair)
        blocks = smoothed.reshape(member_count, row_count, 128)
        summed = jnp.einsum("mk,mrl->rkl", onehot, blocks, precision=lax.Precision.HIGHEST)
        summed = lax.psum_scatter(summed, "bank", scatter_dimension=0, tiled=True)
        summed = lax.psum(summed, "blk")
        center_owned = (summed / counts[None, :, None]).astype(BF16)
        center_all = lax.all_gather(center_owned, "bank", axis=0, tiled=True)
        chosen = jnp.einsum("mk,rkl->mrl", onehot.astype(BF16), center_all, preferred_element_type=F32)
        potential = chosen.reshape(member_count, cell_count) - smoothed
    centers = jnp.transpose(center_owned, (1, 0, 2)).reshape(BARS, center_owned.shape[0] * 128)
    return centers, potential


def solution(mesh):
    groups, banks = mesh.shape["blk"], mesh.shape["bank"]

    def per_device(log_density, assignment):
        rows = G * log_density.shape[0]
        fits = G % banks == 0 and (rows // banks) % 16 == 0 and PLANE % (128 * groups) == 0
        if fits and min(groups, banks) > 1:
            return fused_device(groups, banks, log_density, assignment)
        return plain_device(log_density, assignment)

    placed = (P(("blk", "bank"), None), P(("blk", "bank")))
    return jax.shard_map(
        per_device,
        mesh=mesh,
        in_specs=placed,
        out_specs=(P(None, "bank"), P(("blk", "bank"), None)),
        check_vma=False,
    )
```

```python
import functools

import jax
import jax.numpy as jnp
import ml_dtypes
import numpy as np
from jax import lax
from jax.experimental import pallas as pl
from jax.experimental.pallas import tpu as pltpu
from jax.sharding import PartitionSpec as P

G = 32
PLANE = G * G
BARS = 8
ITERS = 2
MESH = pl.DeviceIdType.MESH
F32 = jnp.float32
BF16 = jnp.bfloat16


def host_tables():
    grid_pos = np.arange(G, dtype=np.float32)
    offset = grid_pos[:, None] - grid_pos[None, :]
    line = np.exp(np.float32(-0.5) * offset * offset)
    pair = (line[:, None, :, None] * line[None, :, None, :]).reshape(PLANE, PLANE).astype(ml_dtypes.bfloat16)
    return line, pair


def kernel(
    groups, banks, members,
    density_hbm, label_hbm, pair_hbm, line_hbm, scale_hbm,
    centers_ref, potential_ref,
    density_ref, label_ref, line_ref, scale_ref, pair, source, running, lifted, smoothed, outgoing, incoming, partial, partial_in, shared, chosen, chosen_in,
    labels, label_out, count_out, count_in,
    load_sem, label_sem, count_sem, member_send, member_recv, partial_sem, shared_send, shared_recv, chosen_send, chosen_recv,
):
    blk, bank = lax.axis_index("blk"), lax.axis_index("bank")
    rows = G * members
    chunk = rows // banks
    slabs = G // banks
    width = PLANE // groups
    kept = slabs * BARS

    def group_at(step):
        return lax.rem(blk + step, groups)

    order = sorted(range(1, banks), key=lambda mask: ((mask == 1) * 4 + (mask // 2 == 1) * 2 + mask % 2, -mask))
    folds = banks & (banks - 1) == 0

    def bank_at(hop):
        if not folds:
            return lax.rem(bank + hop, banks)
        peer, bit = 0, 1
        while bit < banks:
            peer += lax.rem(bank // bit + order[hop - 1] // bit, 2) * bit
            bit *= 2
        return peer

    def chunk_at(index):
        return pl.ds(pl.multiple_of(index * chunk, chunk), chunk)

    def tile_at(step):
        if step == groups - 1:
            return blk
        up = step + (blk <= step).astype(jnp.int32)
        down = groups - 1 - step - (groups - 1 - blk <= step).astype(jnp.int32)
        return jnp.where(2 * blk >= groups, up, down)

    def spread(src, dst, iteration, tile, send_sem, recv_sem):
        for hop in range(1, banks):
            peer = bank_at(hop)
            push(
                src.at[iteration, tile, chunk_at(peer), :], dst.at[iteration, tile, chunk_at(bank), :],
                send_sem.at[iteration], recv_sem.at[iteration, tile], (blk, peer),
            )
        dst[iteration, tile, chunk_at(bank), :] = src[iteration, tile, chunk_at(bank), :]

    def await_spread(dst, iteration, tile, recv_sem):
        await_bytes(dst.at[iteration, tile, 0:rows - chunk, :], recv_sem.at[iteration, tile])

    def push(src, dst, send_sem, recv_sem, device):
        pltpu.make_async_remote_copy(
            src_ref=src, dst_ref=dst, send_sem=send_sem, recv_sem=recv_sem,
            device_id=device, device_id_type=MESH,
        ).start()

    def await_bytes(ref, sem):
        pltpu.make_async_copy(ref, ref, sem).wait()

    loads = [
        pltpu.make_async_copy(src, dst, load_sem.at[index])
        for index, (src, dst) in enumerate((
            (density_hbm, density_ref), (label_hbm, label_ref), (scale_hbm, scale_ref), (line_hbm, line_ref),
        ))
    ]
    for step in range(groups):
        tile = tile_at(step)
        loads.append(pltpu.make_async_copy(pair_hbm.at[tile], pair.at[tile], load_sem.at[4 + step]))
    for load in loads:
        load.start()
    barrier = pltpu.get_barrier_semaphore()
    for step in range(1, banks):
        pl.semaphore_signal(barrier, inc=1, device_id=(blk, bank_at(step)), device_id_type=MESH)
    for step in range(1, groups):
        pl.semaphore_signal(barrier, inc=1, device_id=(group_at(step), bank), device_id_type=MESH)

    loads[1].wait()
    own_rows = lax.broadcasted_iota(jnp.int32, (chunk, 128), 0) % members
    own_labels = jnp.zeros((chunk, 128), F32)
    for member in range(members):
        own_labels = jnp.where(own_rows == member, label_ref[member].astype(F32), own_labels)
    label_out[...] = own_labels.astype(BF16)
    labels[chunk_at(bank), :] = own_labels.astype(BF16)

    loads[0].wait()
    for tile in range(groups):
        for x in range(G):
            lifted[tile, members * x:members * (x + 1), :] = density_ref[
                :, x * PLANE + tile * width:x * PLANE + (tile + 1) * width
            ].astype(F32)
    loads[2].wait()
    for tile in range(groups):
        risen = jnp.exp(lifted[tile])
        lifted[tile] = risen
        for part in range(width // 128):
            column = tile * (width // 128) + part
            scale = scale_ref[:rows, :] * scale_ref[rows + column:rows + column + 1, :]
            source[:, column * 128:(column + 1) * 128] = (risen[:, part * 128:(part + 1) * 128] * scale).astype(BF16)
    loads[3].wait()

    def across(inner):
        high = inner.astype(BF16)
        low = (inner - high.astype(F32)).astype(BF16)
        return jnp.dot(line_ref[...], jnp.concatenate([high, high, low], axis=0), preferred_element_type=F32)

    pick = None
    for iteration in range(ITERS):
        last = iteration == ITERS - 1
        for step in range(groups):
            tile = tile_at(step)
            if iteration == 0:
                loads[4 + step].wait()
            value = jnp.log(across(jnp.dot(source[...], pair[tile], preferred_element_type=F32)))
            smoothed[tile] = value
            outgoing[iteration, tile] = value.astype(BF16)
            if iteration == 0 and step == 0:
                pl.semaphore_wait(barrier, banks - 1 + groups - 1)
            spread(outgoing, incoming, iteration, tile, member_send, member_recv)
            if iteration == 0 and step == 0:
                for hop in range(1, banks):
                    push(label_out, labels.at[chunk_at(bank), :], label_sem.at[0], label_sem.at[1], (blk, bank_at(hop)))

        if iteration == 0:
            await_bytes(labels.at[0:rows - chunk, :], label_sem.at[1])
            row = lax.broadcasted_iota(jnp.int32, (rows, 128), 0)
            lane = lax.broadcasted_iota(jnp.int32, (rows, 128), 1)
            match = (labels[...].astype(F32) == (lane % BARS).astype(F32)) & ((row // members) % slabs == lane // BARS)
            pick_wide = jnp.where(match, 1.0, 0.0).astype(F32)
            gather_wide = jnp.transpose(pick_wide)
            pick = pick_wide.astype(BF16)[:, :kept]
            gather = gather_wide.astype(BF16)[:kept, :]
            own_count = jnp.broadcast_to(jnp.sum(gather_wide[:BARS, :], axis=1, keepdims=True), (BARS, 128))
            count_out[...] = own_count
            count_in[blk] = own_count
            for step in range(1, groups):
                push(count_out, count_in.at[blk], count_sem.at[0], count_sem.at[1], (group_at(step), bank))

        for step in range(groups):
            tile = tile_at(step)
            await_spread(incoming, iteration, tile, member_recv)
            sums = jnp.dot(gather, incoming[iteration, tile], preferred_element_type=F32)
            if step < groups - 1:
                partial[iteration, tile] = sums
                push(
                    partial.at[iteration, tile], partial_in.at[iteration, blk],
                    partial_sem.at[iteration, 0], partial_sem.at[iteration, 1], (tile, bank),
                )
            else:
                partial_in[iteration, blk] = sums

        if iteration == 0:
            await_bytes(count_in.at[0:groups - 1], count_sem.at[1])
            counts = functools.reduce(jnp.add, [count_in[group] for group in range(groups)])
            scale = 1.0 / jnp.concatenate([counts[:, :1]] * slabs, axis=0)
        await_bytes(partial_in.at[iteration, 0:groups - 1], partial_sem.at[iteration, 1])
        total = functools.reduce(jnp.add, [partial_in[iteration, group] for group in range(groups)])
        shared[iteration, blk] = (total * scale).astype(BF16)
        for step in range(groups - 1):
            push(
                shared.at[iteration, blk], shared.at[iteration, blk],
                shared_send.at[iteration], shared_recv.at[iteration, blk], (tile_at(step), bank),
            )

        for step in reversed(range(groups)):
            tile = tile_at(step)
            if step < groups - 1:
                await_bytes(shared.at[iteration, tile], shared_recv.at[iteration, tile])
            center = shared[iteration, tile]
            chosen[iteration, tile] = jnp.dot(pick, center, preferred_element_type=F32).astype(BF16)
            spread(chosen, chosen_in, iteration, tile, chosen_send, chosen_recv)
        if last:
            for tile in range(groups):
                for slab in range(slabs):
                    start = slab * PLANE + tile * width
                    centers_ref[:, start:start + width] = shared[iteration, tile, slab * BARS:(slab + 1) * BARS, :]

        for step in reversed(range(groups)):
            tile = tile_at(step)
            await_spread(chosen_in, iteration, tile, chosen_recv)
            value = chosen_in[iteration, tile].astype(F32) - smoothed[tile]
            if last:
                for x in range(G):
                    start = pl.multiple_of(x * PLANE + tile * width, width)
                    potential_ref[:, pl.ds(start, width)] = value[members * x:members * (x + 1), :]
            else:
                raised = jnp.exp(value).astype(BF16)
                depth = pl.ds(pl.multiple_of(tile * width, width), width)
                for target in range(groups):
                    inner = jnp.dot(raised, pair[target, depth, :], preferred_element_type=F32)
                    if step < groups - 1:
                        inner += running[target]
                    if step:
                        running[target] = inner
                    else:
                        columns = slice(target * width, (target + 1) * width)
                        source[:, columns] = (lifted[target] / across(inner)).astype(BF16)

    for _ in range(banks - 1):
        await_bytes(label_out, label_sem.at[0])
    for _ in range(groups - 1):
        await_bytes(count_out, count_sem.at[0])
    for iteration in range(ITERS):
        await_bytes(outgoing.at[iteration, :, 0:rows - chunk, :], member_send.at[iteration])
        await_bytes(partial.at[iteration, 0:groups - 1], partial_sem.at[iteration, 0])
        await_bytes(shared.at[iteration, 0:groups - 1], shared_send.at[iteration])
        await_bytes(chosen.at[iteration, :, 0:rows - chunk, :], chosen_send.at[iteration])


def store_results(centers_in, potential_in, centers_out, potential_out, sems):
    copies = [
        pltpu.make_async_copy(centers_in, centers_out, sems.at[0]),
        pltpu.make_async_copy(potential_in, potential_out, sems.at[1]),
    ]
    for copy in copies:
        copy.start()
    for copy in copies:
        copy.wait()


def fused_device(groups, banks, log_density, assignment):
    members, cells = log_density.shape
    rows, chunk = G * members, G * members // banks
    width = PLANE // groups
    kept = G // banks * BARS
    line, pair = host_tables()
    tiled_pair = np.ascontiguousarray(pair.reshape(PLANE, groups, width).transpose(1, 0, 2))
    line_rows = np.kron(line, np.eye(members, dtype=np.float32))
    high = line_rows.astype(ml_dtypes.bfloat16)
    low = (line_rows - high.astype(np.float32)).astype(ml_dtypes.bfloat16)
    line_parts = np.concatenate([high, low, high], axis=1)
    row_scale = np.broadcast_to(1.0 / line_rows.sum(axis=1, keepdims=True), (rows, 128))
    column_scale = (1.0 / pair.astype(np.float32).sum(axis=0)).reshape(PLANE // 128, 128)
    scales = np.concatenate([row_scale, column_scale], axis=0).astype(np.float32)
    operands = (log_density, assignment, jnp.asarray(tiled_pair), jnp.asarray(line_parts), jnp.asarray(scales))
    vmem = pl.BlockSpec(memory_space=pltpu.VMEM)
    dma = pltpu.SemaphoreType.DMA
    results = pl.pallas_call(
        functools.partial(kernel, groups, banks, members),
        out_shape=(
            jax.ShapeDtypeStruct((BARS, cells // banks), BF16),
            jax.ShapeDtypeStruct((members, cells), F32),
        ),
        in_specs=[pl.BlockSpec(memory_space=pltpu.HBM)] * 5,
        out_specs=(vmem, vmem),
        scratch_shapes=[
            pltpu.VMEM(log_density.shape, BF16),
            pltpu.SMEM(assignment.shape, jnp.int32),
            pltpu.VMEM(line_parts.shape, BF16),
            pltpu.VMEM(scales.shape, F32),
            pltpu.VMEM((groups, PLANE, width), BF16),
            pltpu.VMEM((rows, PLANE), BF16),
            pltpu.VMEM((groups, rows, width), F32),
            pltpu.VMEM((groups, rows, width), F32),
            pltpu.VMEM((groups, rows, width), F32),
            pltpu.VMEM((ITERS, groups, rows, width), BF16),
            pltpu.VMEM((ITERS, groups, rows, width), BF16),
            pltpu.VMEM((ITERS, groups, kept, width), F32),
            pltpu.VMEM((ITERS, groups, kept, width), F32),
            pltpu.VMEM((ITERS, groups, kept, width), BF16),
            pltpu.VMEM((ITERS, groups, rows, width), BF16),
            pltpu.VMEM((ITERS, groups, rows, width), BF16),
            pltpu.VMEM((rows, 128), BF16),
            pltpu.VMEM((chunk, 128), BF16),
            pltpu.VMEM((BARS, 128), F32),
            pltpu.VMEM((groups, BARS, 128), F32),
            dma((4 + groups,)), dma((2,)), dma((2,)),
            dma((ITERS,)), dma((ITERS, groups)),
            dma((ITERS, 2)),
            dma((ITERS,)), dma((ITERS, groups)),
            dma((ITERS,)), dma((ITERS, groups)),
        ],
        compiler_params=pltpu.CompilerParams(
            collective_id=0, has_side_effects=True, vmem_limit_bytes=40 * 1024 * 1024
        ),
    )(*(pltpu.with_memory_space_constraint(operand, pltpu.HBM) for operand in operands))
    pinned = [pltpu.with_memory_space_constraint(result, pltpu.VMEM) for result in results]
    return pl.pallas_call(
        store_results,
        out_shape=tuple(pltpu.HBM(result.shape, result.dtype) for result in results),
        in_specs=[vmem] * 2,
        out_specs=(pl.BlockSpec(memory_space=pltpu.HBM),) * 2,
        scratch_shapes=[dma((2,))],
    )(*pinned)


def log_convolve(field_log, kernel_line, kernel_pair):
    member_count = field_log.shape[0]
    raised = jnp.exp(field_log).astype(BF16).reshape(member_count * G, PLANE)
    inner_sum = jnp.dot(raised, kernel_pair, preferred_element_type=F32).reshape(member_count, G, PLANE)
    outer_sum = jnp.einsum("ij,mjc->mic", kernel_line, inner_sum, precision=lax.Precision.HIGHEST)
    return jnp.log(outer_sum).reshape(member_count, G * PLANE)


def plain_device(log_density, assignment):
    line, pair = host_tables()
    kernel_line, kernel_pair = jnp.asarray(line), jnp.asarray(pair)
    member_count, cell_count = log_density.shape
    row_count = cell_count // 128
    labels = jnp.arange(BARS, dtype=jnp.int32)
    onehot = (assignment[:, None] == labels[None, :]).astype(F32)
    counts = lax.psum(jnp.sum(onehot, axis=0), ("blk", "bank"))
    potential = jnp.zeros((member_count, cell_count), F32)
    center_owned = None
    for _ in range(ITERS):
        source = log_density.astype(F32) - log_convolve(potential, kernel_line, kernel_pair)
        smoothed = log_convolve(source, kernel_line, kernel_pair)
        blocks = smoothed.reshape(member_count, row_count, 128)
        summed = jnp.einsum("mk,mrl->rkl", onehot, blocks, precision=lax.Precision.HIGHEST)
        summed = lax.psum_scatter(summed, "bank", scatter_dimension=0, tiled=True)
        summed = lax.psum(summed, "blk")
        center_owned = (summed / counts[None, :, None]).astype(BF16)
        center_all = lax.all_gather(center_owned, "bank", axis=0, tiled=True)
        chosen = jnp.einsum("mk,rkl->mrl", onehot.astype(BF16), center_all, preferred_element_type=F32)
        potential = chosen.reshape(member_count, cell_count) - smoothed
    centers = jnp.transpose(center_owned, (1, 0, 2)).reshape(BARS, center_owned.shape[0] * 128)
    return centers, potential


def solution(mesh):
    groups, banks = mesh.shape["blk"], mesh.shape["bank"]

    def per_device(log_density, assignment):
        rows = G * log_density.shape[0]
        fits = G % banks == 0 and (rows // banks) % 16 == 0 and PLANE % (128 * groups) == 0
        if fits and min(groups, banks) > 1:
            return fused_device(groups, banks, log_density, assignment)
        return plain_device(log_density, assignment)

    placed = (P(("blk", "bank"), None), P(("blk", "bank")))
    return jax.shard_map(
        per_device,
        mesh=mesh,
        in_specs=placed,
        out_specs=(P(None, "bank"), P(("blk", "bank"), None)),
        check_vma=False,
    )
```

```python
import functools

import jax
import jax.numpy as jnp
import ml_dtypes
import numpy as np
from jax import lax
from jax.experimental import pallas as pl
from jax.experimental.pallas import tpu as pltpu
from jax.sharding import PartitionSpec as P

G = 32
PLANE = G * G
BARS = 8
ITERS = 2
MESH = pl.DeviceIdType.MESH
F32 = jnp.float32
BF16 = jnp.bfloat16


def host_tables():
    grid_pos = np.arange(G, dtype=np.float32)
    offset = grid_pos[:, None] - grid_pos[None, :]
    line = np.exp(np.float32(-0.5) * offset * offset)
    pair = (line[:, None, :, None] * line[None, :, None, :]).reshape(PLANE, PLANE).astype(ml_dtypes.bfloat16)
    return line, pair


def kernel(
    groups, banks, members,
    density_hbm, label_hbm, pair_hbm, line_hbm, scale_hbm,
    centers_ref, potential_ref,
    density_ref, label_ref, line_ref, scale_ref, pair, source, running, lifted, smoothed, outgoing, incoming, partial, shared, chosen, chosen_in,
    labels, label_out, count_out, count_in,
    load_sem, label_sem, count_sem, member_send, member_recv, partial_send, partial_recv, chosen_send, chosen_recv,
):
    blk, bank = lax.axis_index("blk"), lax.axis_index("bank")
    rows = G * members
    chunk = rows // banks
    slabs = G // banks
    width = PLANE // groups
    kept = slabs * BARS

    order = sorted(range(1, banks), key=lambda mask: ((mask == 1) * 4 + (mask // 2 == 1) * 2 + mask % 2, -mask))
    folds = banks & (banks - 1) == 0

    def bank_at(hop):
        if not folds:
            return lax.rem(bank + hop, banks)
        peer, bit = 0, 1
        while bit < banks:
            peer += lax.rem(bank // bit + order[hop - 1] // bit, 2) * bit
            bit *= 2
        return peer

    def chunk_at(index):
        return pl.ds(pl.multiple_of(index * chunk, chunk), chunk)

    def group_at(step):
        up = step + (blk <= step).astype(jnp.int32)
        down = groups - 1 - step - (groups - 1 - blk <= step).astype(jnp.int32)
        return jnp.where(2 * blk >= groups, up, down)

    def spread(src, dst, iteration, tile, send_sem, recv_sem):
        for hop in range(1, banks):
            peer = bank_at(hop)
            push(
                src.at[iteration, tile, chunk_at(peer), :], dst.at[iteration, tile, chunk_at(bank), :],
                send_sem.at[iteration], recv_sem.at[iteration, tile], (blk, peer),
            )
        dst[iteration, tile, chunk_at(bank), :] = src[iteration, tile, chunk_at(bank), :]

    def await_spread(dst, iteration, tile, recv_sem):
        await_bytes(dst.at[iteration, tile, 0:rows - chunk, :], recv_sem.at[iteration, tile])

    def push(src, dst, send_sem, recv_sem, device):
        pltpu.make_async_remote_copy(
            src_ref=src, dst_ref=dst, send_sem=send_sem, recv_sem=recv_sem,
            device_id=device, device_id_type=MESH,
        ).start()

    def await_bytes(ref, sem):
        pltpu.make_async_copy(ref, ref, sem).wait()

    barrier = pltpu.get_barrier_semaphore()
    for step in range(groups - 1):
        pl.semaphore_signal(barrier, inc=1, device_id=(group_at(step), bank), device_id_type=MESH)
    for hop in range(1, banks):
        pl.semaphore_signal(barrier, inc=1, device_id=(blk, bank_at(hop)), device_id_type=MESH)
    loads = [
        pltpu.make_async_copy(src, dst, load_sem.at[index])
        for index, (src, dst) in enumerate((
            (density_hbm, density_ref), (label_hbm, label_ref), (scale_hbm, scale_ref), (line_hbm, line_ref),
        ))
    ]
    for tile in range(groups):
        loads.append(pltpu.make_async_copy(pair_hbm.at[tile], pair.at[tile], load_sem.at[4 + tile]))
    for load in loads:
        load.start()
    loads[1].wait()
    own_rows = lax.broadcasted_iota(jnp.int32, (chunk, 128), 0) % members
    own_labels = jnp.zeros((chunk, 128), F32)
    for member in range(members):
        own_labels = jnp.where(own_rows == member, label_ref[member].astype(F32), own_labels)
    label_out[...] = own_labels.astype(BF16)
    labels[chunk_at(bank), :] = own_labels.astype(BF16)

    loads[0].wait()
    for tile in range(groups):
        for x in range(G):
            lifted[tile, members * x:members * (x + 1), :] = density_ref[
                :, x * PLANE + tile * width:x * PLANE + (tile + 1) * width
            ].astype(F32)
    loads[2].wait()
    for tile in range(groups):
        risen = jnp.exp(lifted[tile])
        lifted[tile] = risen
        for part in range(width // 128):
            column = tile * (width // 128) + part
            scale = scale_ref[:rows, :] * scale_ref[rows + column:rows + column + 1, :]
            source[:, column * 128:(column + 1) * 128] = (risen[:, part * 128:(part + 1) * 128] * scale).astype(BF16)
    loads[3].wait()

    def across(inner):
        high = inner.astype(BF16)
        low = (inner - high.astype(F32)).astype(BF16)
        return jnp.dot(line_ref[...], jnp.concatenate([high, high, low], axis=0), preferred_element_type=F32)

    pick = None
    for iteration in range(ITERS):
        last = iteration == ITERS - 1
        for tile in range(groups):
            if iteration == 0:
                loads[4 + tile].wait()
            value = jnp.log(across(jnp.dot(source[...], pair[tile], preferred_element_type=F32)))
            smoothed[tile] = value
            outgoing[iteration, tile] = value.astype(BF16)
            if iteration == 0 and tile == 0:
                pl.semaphore_wait(barrier, banks - 1 + groups - 1)
            spread(outgoing, incoming, iteration, tile, member_send, member_recv)
            if iteration == 0 and tile == 0:
                for hop in range(1, banks):
                    push(label_out, labels.at[chunk_at(bank), :], label_sem.at[0], label_sem.at[1], (blk, bank_at(hop)))

        if iteration == 0:
            await_bytes(labels.at[0:rows - chunk, :], label_sem.at[1])
            row = lax.broadcasted_iota(jnp.int32, (rows, 128), 0)
            lane = lax.broadcasted_iota(jnp.int32, (rows, 128), 1)
            match = (labels[...].astype(F32) == (lane % BARS).astype(F32)) & ((row // members) % slabs == lane // BARS)
            pick_wide = jnp.where(match, 1.0, 0.0).astype(F32)
            gather_wide = jnp.transpose(pick_wide)
            pick = pick_wide.astype(BF16)[:, :kept]
            gather = gather_wide.astype(BF16)[:kept, :]
            own_count = jnp.broadcast_to(jnp.sum(gather_wide[:BARS, :], axis=1, keepdims=True), (BARS, 128))
            count_out[...] = own_count
            count_in[blk] = own_count
            own_counts = jnp.concatenate([own_count[:, :1]] * slabs, axis=0)
            for step in range(groups - 1):
                push(count_out, count_in.at[blk], count_sem.at[0], count_sem.at[1], (group_at(step), bank))

        for tile in range(groups):
            await_spread(incoming, iteration, tile, member_recv)
            sums = jnp.dot(gather, incoming[iteration, tile], preferred_element_type=F32)
            if iteration:
                sums -= own_counts * shared[iteration - 1, tile].astype(F32)
            partial[iteration, tile, blk] = sums.astype(BF16)
            for step in range(groups - 1):
                push(
                    partial.at[iteration, tile, blk], partial.at[iteration, tile, blk],
                    partial_send.at[iteration], partial_recv.at[iteration, tile], (group_at(step), bank),
                )

        if iteration == 0:
            await_bytes(count_in.at[0:groups - 1], count_sem.at[1])
            counts = functools.reduce(jnp.add, [count_in[group] for group in range(groups)])
            scale = 1.0 / jnp.concatenate([counts[:, :1]] * slabs, axis=0)
        for tile in range(groups):
            await_bytes(partial.at[iteration, tile, 0:groups - 1], partial_recv.at[iteration, tile])
            total = functools.reduce(jnp.add, [partial[iteration, tile, group].astype(F32) for group in range(groups)])
            center = total * scale
            if iteration:
                center += shared[iteration - 1, tile].astype(F32)
            center = center.astype(BF16)
            shared[iteration, tile] = center
            chosen[iteration, tile] = jnp.dot(pick, center, preferred_element_type=F32).astype(BF16)
            spread(chosen, chosen_in, iteration, tile, chosen_send, chosen_recv)

        if last:
            for tile in range(groups):
                for slab in range(slabs):
                    start = slab * PLANE + tile * width
                    centers_ref[:, start:start + width] = shared[iteration, tile, slab * BARS:(slab + 1) * BARS, :]

        for tile in range(groups):
            await_spread(chosen_in, iteration, tile, chosen_recv)
            value = chosen_in[iteration, tile].astype(F32) - smoothed[tile]
            if last:
                for x in range(G):
                    start = x * PLANE + tile * width
                    potential_ref[:, start:start + width] = value[members * x:members * (x + 1), :]
            else:
                raised = jnp.exp(value).astype(BF16)
                for target in range(groups):
                    inner = jnp.dot(raised, pair[target, tile * width:(tile + 1) * width, :], preferred_element_type=F32)
                    if tile:
                        inner += running[target]
                    if tile < groups - 1:
                        running[target] = inner
                    else:
                        columns = slice(target * width, (target + 1) * width)
                        source[:, columns] = (lifted[target] / across(inner)).astype(BF16)

    for _ in range(banks - 1):
        await_bytes(label_out, label_sem.at[0])
    for _ in range(groups - 1):
        await_bytes(count_out, count_sem.at[0])
    for iteration in range(ITERS):
        await_bytes(outgoing.at[iteration, :, 0:rows - chunk, :], member_send.at[iteration])
        await_bytes(partial.at[iteration, :, 0:groups - 1], partial_send.at[iteration])
        await_bytes(chosen.at[iteration, :, 0:rows - chunk, :], chosen_send.at[iteration])


def store_results(centers_in, potential_in, centers_out, potential_out, sems):
    copies = [
        pltpu.make_async_copy(centers_in, centers_out, sems.at[0]),
        pltpu.make_async_copy(potential_in, potential_out, sems.at[1]),
    ]
    for copy in copies:
        copy.start()
    for copy in copies:
        copy.wait()


def fused_device(groups, banks, log_density, assignment):
    members, cells = log_density.shape
    rows, chunk = G * members, G * members // banks
    width = PLANE // groups
    kept = G // banks * BARS
    line, pair = host_tables()
    tiled_pair = np.ascontiguousarray(pair.reshape(PLANE, groups, width).transpose(1, 0, 2))
    line_rows = np.kron(line, np.eye(members, dtype=np.float32))
    high = line_rows.astype(ml_dtypes.bfloat16)
    low = (line_rows - high.astype(np.float32)).astype(ml_dtypes.bfloat16)
    line_parts = np.concatenate([high, low, high], axis=1)
    row_scale = np.broadcast_to(1.0 / line_rows.sum(axis=1, keepdims=True), (rows, 128))
    column_scale = (1.0 / pair.astype(np.float32).sum(axis=0)).reshape(PLANE // 128, 128)
    scales = np.concatenate([row_scale, column_scale], axis=0).astype(np.float32)
    operands = (log_density, assignment, jnp.asarray(tiled_pair), jnp.asarray(line_parts), jnp.asarray(scales))
    vmem = pl.BlockSpec(memory_space=pltpu.VMEM)
    dma = pltpu.SemaphoreType.DMA
    results = pl.pallas_call(
        functools.partial(kernel, groups, banks, members),
        out_shape=(
            jax.ShapeDtypeStruct((BARS, cells // banks), BF16),
            jax.ShapeDtypeStruct((members, cells), F32),
        ),
        in_specs=[pl.BlockSpec(memory_space=pltpu.HBM)] * 5,
        out_specs=(vmem, vmem),
        scratch_shapes=[
            pltpu.VMEM(log_density.shape, BF16),
            pltpu.SMEM(assignment.shape, jnp.int32),
            pltpu.VMEM(line_parts.shape, BF16),
            pltpu.VMEM(scales.shape, F32),
            pltpu.VMEM((groups, PLANE, width), BF16),
            pltpu.VMEM((rows, PLANE), BF16),
            pltpu.VMEM((groups, rows, width), F32),
            pltpu.VMEM((groups, rows, width), F32),
            pltpu.VMEM((groups, rows, width), F32),
            pltpu.VMEM((ITERS, groups, rows, width), BF16),
            pltpu.VMEM((ITERS, groups, rows, width), BF16),
            pltpu.VMEM((ITERS, groups, groups, kept, width), BF16),
            pltpu.VMEM((ITERS, groups, kept, width), BF16),
            pltpu.VMEM((ITERS, groups, rows, width), BF16),
            pltpu.VMEM((ITERS, groups, rows, width), BF16),
            pltpu.VMEM((rows, 128), BF16),
            pltpu.VMEM((chunk, 128), BF16),
            pltpu.VMEM((BARS, 128), F32),
            pltpu.VMEM((groups, BARS, 128), F32),
            dma((4 + groups,)), dma((2,)), dma((2,)),
            dma((ITERS,)), dma((ITERS, groups)),
            dma((ITERS,)), dma((ITERS, groups)),
            dma((ITERS,)), dma((ITERS, groups)),
        ],
        compiler_params=pltpu.CompilerParams(
            collective_id=0, has_side_effects=True, vmem_limit_bytes=40 * 1024 * 1024
        ),
    )(*(pltpu.with_memory_space_constraint(operand, pltpu.HBM) for operand in operands))
    pinned = [pltpu.with_memory_space_constraint(result, pltpu.VMEM) for result in results]
    return pl.pallas_call(
        store_results,
        out_shape=tuple(pltpu.HBM(result.shape, result.dtype) for result in results),
        in_specs=[vmem] * 2,
        out_specs=(pl.BlockSpec(memory_space=pltpu.HBM),) * 2,
        scratch_shapes=[dma((2,))],
    )(*pinned)


def log_convolve(field_log, kernel_line, kernel_pair):
    member_count = field_log.shape[0]
    raised = jnp.exp(field_log).astype(BF16).reshape(member_count * G, PLANE)
    inner_sum = jnp.dot(raised, kernel_pair, preferred_element_type=F32).reshape(member_count, G, PLANE)
    outer_sum = jnp.einsum("ij,mjc->mic", kernel_line, inner_sum, precision=lax.Precision.HIGHEST)
    return jnp.log(outer_sum).reshape(member_count, G * PLANE)


def plain_device(log_density, assignment):
    line, pair = host_tables()
    kernel_line, kernel_pair = jnp.asarray(line), jnp.asarray(pair)
    member_count, cell_count = log_density.shape
    row_count = cell_count // 128
    labels = jnp.arange(BARS, dtype=jnp.int32)
    onehot = (assignment[:, None] == labels[None, :]).astype(F32)
    counts = lax.psum(jnp.sum(onehot, axis=0), ("blk", "bank"))
    potential = jnp.zeros((member_count, cell_count), F32)
    center_owned = None
    for _ in range(ITERS):
        source = log_density.astype(F32) - log_convolve(potential, kernel_line, kernel_pair)
        smoothed = log_convolve(source, kernel_line, kernel_pair)
        blocks = smoothed.reshape(member_count, row_count, 128)
        summed = jnp.einsum("mk,mrl->rkl", onehot, blocks, precision=lax.Precision.HIGHEST)
        summed = lax.psum_scatter(summed, "bank", scatter_dimension=0, tiled=True)
        summed = lax.psum(summed, "blk")
        center_owned = (summed / counts[None, :, None]).astype(BF16)
        center_all = lax.all_gather(center_owned, "bank", axis=0, tiled=True)
        chosen = jnp.einsum("mk,rkl->mrl", onehot.astype(BF16), center_all, preferred_element_type=F32)
        potential = chosen.reshape(member_count, cell_count) - smoothed
    centers = jnp.transpose(center_owned, (1, 0, 2)).reshape(BARS, center_owned.shape[0] * 128)
    return centers, potential


def solution(mesh):
    groups, banks = mesh.shape["blk"], mesh.shape["bank"]

    def per_device(log_density, assignment):
        rows = G * log_density.shape[0]
        fits = G % banks == 0 and (rows // banks) % 16 == 0 and PLANE % (128 * groups) == 0
        if fits and min(groups, banks) > 1:
            return fused_device(groups, banks, log_density, assignment)
        return plain_device(log_density, assignment)

    placed = (P(("blk", "bank"), None), P(("blk", "bank")))
    return jax.shard_map(
        per_device,
        mesh=mesh,
        in_specs=placed,
        out_specs=(P(None, "bank"), P(("blk", "bank"), None)),
        check_vma=False,
    )
```

```python
import functools

import jax
import jax.numpy as jnp
import ml_dtypes
import numpy as np
from jax import lax
from jax.experimental import pallas as pl
from jax.experimental.pallas import tpu as pltpu
from jax.sharding import PartitionSpec as P

G = 32
PLANE = G * G
BARS = 8
ITERS = 2
MESH = pl.DeviceIdType.MESH
F32 = jnp.float32
BF16 = jnp.bfloat16


def host_tables():
    grid_pos = np.arange(G, dtype=np.float32)
    offset = grid_pos[:, None] - grid_pos[None, :]
    line = np.exp(np.float32(-0.5) * offset * offset)
    pair = (line[:, None, :, None] * line[None, :, None, :]).reshape(PLANE, PLANE).astype(ml_dtypes.bfloat16)
    return line, pair


def kernel(
    groups, banks, members,
    density_hbm, label_hbm, pair_hbm, line_hbm, scale_hbm,
    centers_ref, potential_ref,
    density_ref, label_ref, line_ref, scale_ref, pair, source, running, lifted, smoothed, outgoing, incoming, partial, shared, shared_in, chosen, chosen_in,
    labels, label_out, count_out, count_in,
    load_sem, label_sem, count_sem, shared_sem, member_send, member_recv, partial_send, partial_recv, chosen_send, chosen_recv,
):
    blk, bank = lax.axis_index("blk"), lax.axis_index("bank")
    rows = G * members
    chunk = rows // banks
    slabs = G // banks
    width = PLANE // groups
    kept = slabs * BARS

    order = sorted(range(1, banks), key=lambda mask: ((mask == 1) * 4 + (mask // 2 == 1) * 2 + mask % 2, -mask))
    folds = banks & (banks - 1) == 0

    def bank_at(hop):
        if hop == 0:
            return bank
        if not folds:
            return lax.rem(bank + hop, banks)
        peer, bit = 0, 1
        while bit < banks:
            peer += lax.rem(bank // bit + order[hop - 1] // bit, 2) * bit
            bit *= 2
        return peer

    def chunk_at(index):
        return pl.ds(pl.multiple_of(index * chunk, chunk), chunk)

    side = lax.rem(blk, 2)
    pair_at = blk // 2
    pairs = groups // 2
    facing = blk + 1 - 2 * side

    def own_tile(index):
        return side * pairs + index

    def facing_tile(index):
        return (1 - side) * pairs + index

    def tile_at(step):
        return own_tile(step // 2) if step % 2 else facing_tile(step // 2)

    def partner_at(step):
        return lax.rem(blk + 2 * step, groups)

    order = sorted(range(1, banks), key=lambda mask: ((mask == 1) * 4 + (mask // 2 == 1) * 2 + mask % 2, -mask))
    folds = banks & (banks - 1) == 0

    def bank_at(hop):
        if hop == 0:
            return bank
        if not folds:
            return lax.rem(bank + hop, banks)
        peer, bit = 0, 1
        while bit < banks:
            peer += lax.rem(bank // bit + order[hop - 1] // bit, 2) * bit
            bit *= 2
        return peer

    def chunk_at(index):
        return pl.ds(pl.multiple_of(index * chunk, chunk), chunk)

    def group_at(step):
        up = step + (blk <= step).astype(jnp.int32)
        down = groups - 1 - step - (groups - 1 - blk <= step).astype(jnp.int32)
        return jnp.where(2 * blk >= groups, up, down)

    def chunk_of(plane_side, index):
        return pl.ds(pl.multiple_of(plane_side * rows + index * chunk, chunk), chunk)

    def push(src, dst, send_sem, recv_sem, device):
        pltpu.make_async_remote_copy(
            src_ref=src, dst_ref=dst, send_sem=send_sem, recv_sem=recv_sem,
            device_id=device, device_id_type=MESH,
        ).start()

    def await_bytes(ref, sem):
        pltpu.make_async_copy(ref, ref, sem).wait()

    barrier = pltpu.get_barrier_semaphore()
    for hop in range(banks):
        pl.semaphore_signal(barrier, inc=1, device_id=(facing, bank_at(hop)), device_id_type=MESH)
    for step in range(1, pairs):
        pl.semaphore_signal(barrier, inc=1, device_id=(partner_at(step), bank), device_id_type=MESH)
    for hop in range(1, banks):
        pl.semaphore_signal(barrier, inc=1, device_id=(blk, bank_at(hop)), device_id_type=MESH)
    loads = [
        pltpu.make_async_copy(src, dst, load_sem.at[index])
        for index, (src, dst) in enumerate((
            (density_hbm, density_ref), (label_hbm, label_ref), (scale_hbm, scale_ref), (line_hbm, line_ref),
        ))
    ]
    for step in range(groups):
        tile = tile_at(step)
        loads.append(pltpu.make_async_copy(pair_hbm.at[tile], pair.at[tile], load_sem.at[4 + step]))
    for load in loads:
        load.start()
    loads[1].wait()
    own_rows = lax.broadcasted_iota(jnp.int32, (chunk, 128), 0) % members
    own_labels = jnp.zeros((chunk, 128), F32)
    for member in range(members):
        own_labels = jnp.where(own_rows == member, label_ref[member].astype(F32), own_labels)
    label_out[...] = own_labels.astype(BF16)
    labels[chunk_of(side, bank), :] = own_labels.astype(BF16)

    loads[0].wait()
    for tile in range(groups):
        for x in range(G):
            lifted[tile, members * x:members * (x + 1), :] = density_ref[
                :, x * PLANE + tile * width:x * PLANE + (tile + 1) * width
            ].astype(F32)
    loads[2].wait()
    for tile in range(groups):
        risen = jnp.exp(lifted[tile])
        lifted[tile] = risen
        for part in range(width // 128):
            column = tile * (width // 128) + part
            scale = scale_ref[:rows, :] * scale_ref[rows + column:rows + column + 1, :]
            source[:, column * 128:(column + 1) * 128] = (risen[:, part * 128:(part + 1) * 128] * scale).astype(BF16)
    loads[3].wait()

    def across(inner):
        high = inner.astype(BF16)
        low = (inner - high.astype(F32)).astype(BF16)
        return jnp.dot(line_ref[...], jnp.concatenate([high, high, low], axis=0), preferred_element_type=F32)

    pick = None
    for iteration in range(ITERS):
        last = iteration == ITERS - 1
        for step in range(groups):
            tile = tile_at(step)
            if iteration == 0:
                loads[4 + step].wait()
            value = jnp.log(across(jnp.dot(source[...], pair[tile], preferred_element_type=F32)))
            smoothed[tile] = value
            outgoing[iteration, tile] = value.astype(BF16)
            if iteration == 0 and step == 0:
                pl.semaphore_wait(barrier, 2 * banks - 1 + pairs - 1)
            own = step % 2
            for hop in range(own, banks):
                peer = bank_at(hop)
                push(
                    outgoing.at[iteration, tile, chunk_at(peer), :],
                    incoming.at[iteration, step // 2, chunk_of(side, bank), :],
                    member_send.at[iteration], member_recv.at[iteration, step // 2], (blk if own else facing, peer),
                )
            if own:
                incoming[iteration, step // 2, chunk_of(side, bank), :] = outgoing[iteration, tile, chunk_at(bank), :]
            if iteration == 0 and step == 0:
                for plane, start in ((facing, 0), (blk, 1)):
                    for hop in range(start, banks):
                        push(
                            label_out, labels.at[chunk_of(side, bank), :],
                            label_sem.at[0], label_sem.at[1], (plane, bank_at(hop)),
                        )

        if iteration == 0:
            await_bytes(labels.at[0:2 * rows - chunk, :], label_sem.at[1])
            row = lax.broadcasted_iota(jnp.int32, (2 * rows, 128), 0)
            lane = lax.broadcasted_iota(jnp.int32, (2 * rows, 128), 1)
            match = (labels[...].astype(F32) == (lane % BARS).astype(F32)) & ((row // members) % slabs == lane // BARS)
            pick_wide = jnp.where(match, 1.0, 0.0).astype(F32)
            gather_wide = jnp.transpose(pick_wide)
            pick = pick_wide.astype(BF16)[:, :kept]
            gather = gather_wide.astype(BF16)[:kept, :]
            own_count = jnp.broadcast_to(jnp.sum(gather_wide[:BARS, :], axis=1, keepdims=True), (BARS, 128))
            count_out[...] = own_count
            count_in[pair_at] = own_count
            own_counts = jnp.concatenate([own_count[:, :1]] * slabs, axis=0)
            for step in range(1, pairs):
                push(count_out, count_in.at[pair_at], count_sem.at[0], count_sem.at[1], (partner_at(step), bank))

        for index in range(pairs):
            await_bytes(incoming.at[iteration, index, 0:2 * rows - chunk, :], member_recv.at[iteration, index])
            sums = jnp.dot(gather, incoming[iteration, index], preferred_element_type=F32)
            if iteration:
                sums -= own_counts * shared[iteration - 1, index].astype(F32)
            partial[iteration, index, pair_at] = sums.astype(BF16)
            for step in range(1, pairs):
                push(
                    partial.at[iteration, index, pair_at], partial.at[iteration, index, pair_at],
                    partial_send.at[iteration], partial_recv.at[iteration, index], (partner_at(step), bank),
                )

        if iteration == 0:
            await_bytes(count_in.at[0:pairs - 1], count_sem.at[1])
            counts = functools.reduce(jnp.add, [count_in[other] for other in range(pairs)])
            scale = 1.0 / jnp.concatenate([counts[:, :1]] * slabs, axis=0)
        for index in range(pairs):
            await_bytes(partial.at[iteration, index, 0:pairs - 1], partial_recv.at[iteration, index])
            total = functools.reduce(jnp.add, [partial[iteration, index, other].astype(F32) for other in range(pairs)])
            center = total * scale
            if iteration:
                center += shared[iteration - 1, index].astype(F32)
            center = center.astype(BF16)
            shared[iteration, index] = center
            chosen[iteration, index] = jnp.dot(pick, center, preferred_element_type=F32).astype(BF16)
            tile = own_tile(index)
            for plane, plane_side, start in ((facing, 1 - side, 0), (blk, side, 1)):
                for hop in range(start, banks):
                    peer = bank_at(hop)
                    push(
                        chosen.at[iteration, index, chunk_of(plane_side, peer), :],
                        chosen_in.at[iteration, tile, chunk_at(bank), :],
                        chosen_send.at[iteration], chosen_recv.at[iteration, tile], (plane, peer),
                    )
            chosen_in[iteration, tile, chunk_at(bank), :] = chosen[iteration, index, chunk_of(side, bank), :]
            if last:
                push(shared.at[iteration, index], shared_in.at[index], shared_sem.at[0], shared_sem.at[1], (facing, bank))

        if last:
            await_bytes(shared_in, shared_sem.at[1])
            for index in range(pairs):
                for tile, found in ((own_tile(index), shared[iteration, index]), (facing_tile(index), shared_in[index])):
                    for slab in range(slabs):
                        start = pl.multiple_of(slab * PLANE + tile * width, width)
                        centers_ref[:, pl.ds(start, width)] = found[slab * BARS:(slab + 1) * BARS, :]

        for step in range(groups):
            own = 1 - step % 2
            tile = own_tile(step // 2) if own else facing_tile(step // 2)
            await_bytes(chosen_in.at[iteration, tile, 0:rows - own * chunk, :], chosen_recv.at[iteration, tile])
            value = chosen_in[iteration, tile].astype(F32) - smoothed[tile]
            if last:
                for x in range(G):
                    start = pl.multiple_of(x * PLANE + tile * width, width)
                    potential_ref[:, pl.ds(start, width)] = value[members * x:members * (x + 1), :]
            else:
                raised = jnp.exp(value).astype(BF16)
                depth = pl.ds(pl.multiple_of(tile * width, width), width)
                for target in range(groups):
                    inner = jnp.dot(raised, pair[target, depth, :], preferred_element_type=F32)
                    if step:
                        inner += running[target]
                    if step < groups - 1:
                        running[target] = inner
                    else:
                        columns = slice(target * width, (target + 1) * width)
                        source[:, columns] = (lifted[target] / across(inner)).astype(BF16)

    for _ in range(2 * banks - 1):
        await_bytes(label_out, label_sem.at[0])
    for _ in range(pairs - 1):
        await_bytes(count_out, count_sem.at[0])
    await_bytes(shared_in, shared_sem.at[0])
    for iteration in range(ITERS):
        await_bytes(incoming.at[iteration, :, 0:2 * rows - chunk, :], member_send.at[iteration])
        await_bytes(partial.at[iteration, :, 0:pairs - 1], partial_send.at[iteration])
        await_bytes(chosen.at[iteration, :, 0:2 * rows - chunk, :], chosen_send.at[iteration])


def store_results(centers_in, potential_in, centers_out, potential_out, sems):
    copies = [
        pltpu.make_async_copy(centers_in, centers_out, sems.at[0]),
        pltpu.make_async_copy(potential_in, potential_out, sems.at[1]),
    ]
    for copy in copies:
        copy.start()
    for copy in copies:
        copy.wait()


def fused_device(groups, banks, log_density, assignment):
    members, cells = log_density.shape
    rows, chunk = G * members, G * members // banks
    width = PLANE // groups
    pairs = groups // 2
    kept = G // banks * BARS
    line, pair = host_tables()
    tiled_pair = np.ascontiguousarray(pair.reshape(PLANE, groups, width).transpose(1, 0, 2))
    line_rows = np.kron(line, np.eye(members, dtype=np.float32))
    high = line_rows.astype(ml_dtypes.bfloat16)
    low = (line_rows - high.astype(np.float32)).astype(ml_dtypes.bfloat16)
    line_parts = np.concatenate([high, low, high], axis=1)
    row_scale = np.broadcast_to(1.0 / line_rows.sum(axis=1, keepdims=True), (rows, 128))
    column_scale = (1.0 / pair.astype(np.float32).sum(axis=0)).reshape(PLANE // 128, 128)
    scales = np.concatenate([row_scale, column_scale], axis=0).astype(np.float32)
    operands = (log_density, assignment, jnp.asarray(tiled_pair), jnp.asarray(line_parts), jnp.asarray(scales))
    vmem = pl.BlockSpec(memory_space=pltpu.VMEM)
    dma = pltpu.SemaphoreType.DMA
    results = pl.pallas_call(
        functools.partial(kernel, groups, banks, members),
        out_shape=(
            jax.ShapeDtypeStruct((BARS, cells // banks), BF16),
            jax.ShapeDtypeStruct((members, cells), F32),
        ),
        in_specs=[pl.BlockSpec(memory_space=pltpu.HBM)] * 5,
        out_specs=(vmem, vmem),
        scratch_shapes=[
            pltpu.VMEM(log_density.shape, BF16),
            pltpu.SMEM(assignment.shape, jnp.int32),
            pltpu.VMEM(line_parts.shape, BF16),
            pltpu.VMEM(scales.shape, F32),
            pltpu.VMEM((groups, PLANE, width), BF16),
            pltpu.VMEM((rows, PLANE), BF16),
            pltpu.VMEM((groups, rows, width), F32),
            pltpu.VMEM((groups, rows, width), F32),
            pltpu.VMEM((groups, rows, width), F32),
            pltpu.VMEM((ITERS, groups, rows, width), BF16),
            pltpu.VMEM((ITERS, pairs, 2 * rows, width), BF16),
            pltpu.VMEM((ITERS, pairs, pairs, kept, width), BF16),
            pltpu.VMEM((ITERS, pairs, kept, width), BF16),
            pltpu.VMEM((pairs, kept, width), BF16),
            pltpu.VMEM((ITERS, pairs, 2 * rows, width), BF16),
            pltpu.VMEM((ITERS, groups, rows, width), BF16),
            pltpu.VMEM((2 * rows, 128), BF16),
            pltpu.VMEM((chunk, 128), BF16),
            pltpu.VMEM((BARS, 128), F32),
            pltpu.VMEM((pairs, BARS, 128), F32),
            dma((4 + groups,)), dma((2,)), dma((2,)), dma((2,)),
            dma((ITERS,)), dma((ITERS, pairs)),
            dma((ITERS,)), dma((ITERS, pairs)),
            dma((ITERS,)), dma((ITERS, groups)),
        ],
        compiler_params=pltpu.CompilerParams(
            collective_id=0, has_side_effects=True, vmem_limit_bytes=40 * 1024 * 1024
        ),
    )(*(pltpu.with_memory_space_constraint(operand, pltpu.HBM) for operand in operands))
    pinned = [pltpu.with_memory_space_constraint(result, pltpu.VMEM) for result in results]
    return pl.pallas_call(
        store_results,
        out_shape=tuple(pltpu.HBM(result.shape, result.dtype) for result in results),
        in_specs=[vmem] * 2,
        out_specs=(pl.BlockSpec(memory_space=pltpu.HBM),) * 2,
        scratch_shapes=[dma((2,))],
    )(*pinned)


def log_convolve(field_log, kernel_line, kernel_pair):
    member_count = field_log.shape[0]
    raised = jnp.exp(field_log).astype(BF16).reshape(member_count * G, PLANE)
    inner_sum = jnp.dot(raised, kernel_pair, preferred_element_type=F32).reshape(member_count, G, PLANE)
    outer_sum = jnp.einsum("ij,mjc->mic", kernel_line, inner_sum, precision=lax.Precision.HIGHEST)
    return jnp.log(outer_sum).reshape(member_count, G * PLANE)


def plain_device(log_density, assignment):
    line, pair = host_tables()
    kernel_line, kernel_pair = jnp.asarray(line), jnp.asarray(pair)
    member_count, cell_count = log_density.shape
    row_count = cell_count // 128
    labels = jnp.arange(BARS, dtype=jnp.int32)
    onehot = (assignment[:, None] == labels[None, :]).astype(F32)
    counts = lax.psum(jnp.sum(onehot, axis=0), ("blk", "bank"))
    potential = jnp.zeros((member_count, cell_count), F32)
    center_owned = None
    for _ in range(ITERS):
        source = log_density.astype(F32) - log_convolve(potential, kernel_line, kernel_pair)
        smoothed = log_convolve(source, kernel_line, kernel_pair)
        blocks = smoothed.reshape(member_count, row_count, 128)
        summed = jnp.einsum("mk,mrl->rkl", onehot, blocks, precision=lax.Precision.HIGHEST)
        summed = lax.psum_scatter(summed, "bank", scatter_dimension=0, tiled=True)
        summed = lax.psum(summed, "blk")
        center_owned = (summed / counts[None, :, None]).astype(BF16)
        center_all = lax.all_gather(center_owned, "bank", axis=0, tiled=True)
        chosen = jnp.einsum("mk,rkl->mrl", onehot.astype(BF16), center_all, preferred_element_type=F32)
        potential = chosen.reshape(member_count, cell_count) - smoothed
    centers = jnp.transpose(center_owned, (1, 0, 2)).reshape(BARS, center_owned.shape[0] * 128)
    return centers, potential


def solution(mesh):
    groups, banks = mesh.shape["blk"], mesh.shape["bank"]

    def per_device(log_density, assignment):
        rows = G * log_density.shape[0]
        fits = G % banks == 0 and (rows // banks) % 16 == 0 and PLANE % (128 * groups) == 0
        if fits and groups % 2 == 0 and groups > 2 and banks > 1:
            return fused_device(groups, banks, log_density, assignment)
        return plain_device(log_density, assignment)

    placed = (P(("blk", "bank"), None), P(("blk", "bank")))
    return jax.shard_map(
        per_device,
        mesh=mesh,
        in_specs=placed,
        out_specs=(P(None, "bank"), P(("blk", "bank"), None)),
        check_vma=False,
    )
```

```python
import functools

import jax
import jax.numpy as jnp
import ml_dtypes
import numpy as np
from jax import lax
from jax.experimental import pallas as pl
from jax.experimental.pallas import tpu as pltpu
from jax.sharding import PartitionSpec as P

G = 32
PLANE = G * G
BARS = 8
ITERS = 2
MESH = pl.DeviceIdType.MESH
F32 = jnp.float32
BF16 = jnp.bfloat16


def host_tables():
    grid_pos = np.arange(G, dtype=np.float32)
    offset = grid_pos[:, None] - grid_pos[None, :]
    line = np.exp(np.float32(-0.5) * offset * offset)
    pair = (line[:, None, :, None] * line[None, :, None, :]).reshape(PLANE, PLANE).astype(ml_dtypes.bfloat16)
    return line, pair


def kernel(
    groups, banks, members,
    density_hbm, label_hbm, pair_hbm, line_hbm, scale_hbm,
    centers_ref, potential_ref,
    density_ref, label_ref, line_ref, scale_ref, pair, source, running, lifted, smoothed, outgoing, incoming, partial, shared, shared_in, chosen, chosen_in,
    labels, label_out, count_out, count_in,
    load_sem, label_sem, count_sem, shared_sem, member_send, member_recv, partial_send, partial_recv, chosen_send, chosen_recv,
):
    blk, bank = lax.axis_index("blk"), lax.axis_index("bank")
    rows = G * members
    chunk = rows // banks
    slabs = G // banks
    width = PLANE // groups
    kept = slabs * BARS

    order = sorted(range(1, banks), key=lambda mask: ((mask == 1) * 4 + (mask // 2 == 1) * 2 + mask % 2, -mask))
    folds = banks & (banks - 1) == 0

    def bank_at(hop):
        if hop == 0:
            return bank
        if not folds:
            return lax.rem(bank + hop, banks)
        peer, bit = 0, 1
        while bit < banks:
            peer += lax.rem(bank // bit + order[hop - 1] // bit, 2) * bit
            bit *= 2
        return peer

    def chunk_at(index):
        return pl.ds(pl.multiple_of(index * chunk, chunk), chunk)

    side = lax.rem(blk, 2)
    pair_at = blk // 2
    pairs = groups // 2
    facing = blk + 1 - 2 * side

    def own_tile(index):
        return side * pairs + index

    def facing_tile(index):
        return (1 - side) * pairs + index

    def tile_at(step):
        return own_tile(step // 2) if step % 2 else facing_tile(step // 2)

    def partner_at(step):
        return lax.rem(blk + 2 * step, groups)

    order = sorted(range(1, banks), key=lambda mask: ((mask == 1) * 4 + (mask // 2 == 1) * 2 + mask % 2, -mask))
    folds = banks & (banks - 1) == 0

    def bank_at(hop):
        if hop == 0:
            return bank
        if not folds:
            return lax.rem(bank + hop, banks)
        peer, bit = 0, 1
        while bit < banks:
            peer += lax.rem(bank // bit + order[hop - 1] // bit, 2) * bit
            bit *= 2
        return peer

    def chunk_at(index):
        return pl.ds(pl.multiple_of(index * chunk, chunk), chunk)

    def group_at(step):
        up = step + (blk <= step).astype(jnp.int32)
        down = groups - 1 - step - (groups - 1 - blk <= step).astype(jnp.int32)
        return jnp.where(2 * blk >= groups, up, down)

    def chunk_of(plane_side, index):
        return pl.ds(pl.multiple_of(plane_side * rows + index * chunk, chunk), chunk)

    def push(src, dst, send_sem, recv_sem, device):
        pltpu.make_async_remote_copy(
            src_ref=src, dst_ref=dst, send_sem=send_sem, recv_sem=recv_sem,
            device_id=device, device_id_type=MESH,
        ).start()

    def await_bytes(ref, sem):
        pltpu.make_async_copy(ref, ref, sem).wait()

    barrier = pltpu.get_barrier_semaphore()
    for hop in range(banks):
        pl.semaphore_signal(barrier, inc=1, device_id=(facing, bank_at(hop)), device_id_type=MESH)
    for step in range(1, pairs):
        pl.semaphore_signal(barrier, inc=1, device_id=(partner_at(step), bank), device_id_type=MESH)
    for hop in range(1, banks):
        pl.semaphore_signal(barrier, inc=1, device_id=(blk, bank_at(hop)), device_id_type=MESH)
    loads = [
        pltpu.make_async_copy(src, dst, load_sem.at[index])
        for index, (src, dst) in enumerate((
            (density_hbm, density_ref), (label_hbm, label_ref), (scale_hbm, scale_ref), (line_hbm, line_ref),
        ))
    ]
    for step in range(groups):
        tile = tile_at(step)
        loads.append(pltpu.make_async_copy(pair_hbm.at[tile], pair.at[tile], load_sem.at[4 + step]))
    for load in loads:
        load.start()
    loads[1].wait()
    own_rows = lax.broadcasted_iota(jnp.int32, (chunk, 128), 0) % members
    own_labels = jnp.zeros((chunk, 128), F32)
    for member in range(members):
        own_labels = jnp.where(own_rows == member, label_ref[member].astype(F32), own_labels)
    label_out[...] = own_labels.astype(BF16)
    labels[chunk_of(side, bank), :] = own_labels.astype(BF16)

    loads[0].wait()
    for tile in range(groups):
        for x in range(G):
            lifted[tile, members * x:members * (x + 1), :] = density_ref[
                :, x * PLANE + tile * width:x * PLANE + (tile + 1) * width
            ].astype(F32)
    loads[2].wait()
    for tile in range(groups):
        risen = jnp.exp(lifted[tile])
        lifted[tile] = risen
        for part in range(width // 128):
            column = tile * (width // 128) + part
            scale = scale_ref[:rows, :] * scale_ref[rows + column:rows + column + 1, :]
            source[:, column * 128:(column + 1) * 128] = (risen[:, part * 128:(part + 1) * 128] * scale).astype(BF16)
    loads[3].wait()

    def across(inner):
        high = inner.astype(BF16)
        low = (inner - high.astype(F32)).astype(BF16)
        return jnp.dot(line_ref[...], jnp.concatenate([high, high, low], axis=0), preferred_element_type=F32)

    pick = None
    for iteration in range(ITERS):
        last = iteration == ITERS - 1
        for step in range(groups):
            tile = tile_at(step)
            if iteration == 0:
                loads[4 + step].wait()
            value = jnp.log(across(jnp.dot(source[...], pair[tile], preferred_element_type=F32)))
            smoothed[tile] = value
            outgoing[iteration, tile] = value.astype(BF16)
            if iteration == 0 and step == 0:
                pl.semaphore_wait(barrier, 2 * banks - 1 + pairs - 1)
            own = step % 2
            for hop in range(own, banks):
                peer = bank_at(hop)
                push(
                    outgoing.at[iteration, tile, chunk_at(peer), :],
                    incoming.at[iteration, step // 2, chunk_of(side, bank), :],
                    member_send.at[iteration], member_recv.at[iteration, step // 2], (blk if own else facing, peer),
                )
            if own:
                incoming[iteration, step // 2, chunk_of(side, bank), :] = outgoing[iteration, tile, chunk_at(bank), :]
            if iteration == 0 and step == 1:
                for plane, start in ((facing, 0), (blk, 1)):
                    for hop in range(start, banks):
                        push(
                            label_out, labels.at[chunk_of(side, bank), :],
                            label_sem.at[0], label_sem.at[1], (plane, bank_at(hop)),
                        )

        if iteration == 0:
            await_bytes(labels.at[0:2 * rows - chunk, :], label_sem.at[1])
            row = lax.broadcasted_iota(jnp.int32, (2 * rows, 128), 0)
            lane = lax.broadcasted_iota(jnp.int32, (2 * rows, 128), 1)
            match = (labels[...].astype(F32) == (lane % BARS).astype(F32)) & ((row // members) % slabs == lane // BARS)
            pick_wide = jnp.where(match, 1.0, 0.0).astype(F32)
            gather_wide = jnp.transpose(pick_wide)
            pick = pick_wide.astype(BF16)[:, :kept]
            gather = gather_wide.astype(BF16)[:kept, :]
            own_count = jnp.broadcast_to(jnp.sum(gather_wide[:BARS, :], axis=1, keepdims=True), (BARS, 128))
            count_out[...] = own_count
            count_in[pair_at] = own_count
            own_counts = jnp.concatenate([own_count[:, :1]] * slabs, axis=0)
            for step in range(1, pairs):
                push(count_out, count_in.at[pair_at], count_sem.at[0], count_sem.at[1], (partner_at(step), bank))

        for index in range(pairs):
            await_bytes(incoming.at[iteration, index, 0:2 * rows - chunk, :], member_recv.at[iteration, index])
            sums = jnp.dot(gather, incoming[iteration, index], preferred_element_type=F32)
            if iteration:
                sums -= own_counts * shared[iteration - 1, index].astype(F32)
            partial[iteration, index, pair_at] = sums.astype(BF16)
            for step in range(1, pairs):
                push(
                    partial.at[iteration, index, pair_at], partial.at[iteration, index, pair_at],
                    partial_send.at[iteration], partial_recv.at[iteration, index], (partner_at(step), bank),
                )

        if iteration == 0:
            await_bytes(count_in.at[0:pairs - 1], count_sem.at[1])
            counts = functools.reduce(jnp.add, [count_in[other] for other in range(pairs)])
            scale = 1.0 / jnp.concatenate([counts[:, :1]] * slabs, axis=0)
        for index in range(pairs):
            await_bytes(partial.at[iteration, index, 0:pairs - 1], partial_recv.at[iteration, index])
            total = functools.reduce(jnp.add, [partial[iteration, index, other].astype(F32) for other in range(pairs)])
            center = total * scale
            if iteration:
                center += shared[iteration - 1, index].astype(F32)
            center = center.astype(BF16)
            shared[iteration, index] = center
            chosen[iteration, index] = jnp.dot(pick, center, preferred_element_type=F32).astype(BF16)
            tile = own_tile(index)
            for plane, plane_side, start in ((facing, 1 - side, 0), (blk, side, 1)):
                for hop in range(start, banks):
                    peer = bank_at(hop)
                    push(
                        chosen.at[iteration, index, chunk_of(plane_side, peer), :],
                        chosen_in.at[iteration, tile, chunk_at(bank), :],
                        chosen_send.at[iteration], chosen_recv.at[iteration, tile], (plane, peer),
                    )
            chosen_in[iteration, tile, chunk_at(bank), :] = chosen[iteration, index, chunk_of(side, bank), :]
            if last:
                push(shared.at[iteration, index], shared_in.at[index], shared_sem.at[0], shared_sem.at[1], (facing, bank))

        if last:
            await_bytes(shared_in, shared_sem.at[1])
            for index in range(pairs):
                for tile, found in ((own_tile(index), shared[iteration, index]), (facing_tile(index), shared_in[index])):
                    for slab in range(slabs):
                        start = pl.multiple_of(slab * PLANE + tile * width, width)
                        centers_ref[:, pl.ds(start, width)] = found[slab * BARS:(slab + 1) * BARS, :]

        for step in range(groups):
            own = 1 - step % 2
            tile = own_tile(step // 2) if own else facing_tile(step // 2)
            await_bytes(chosen_in.at[iteration, tile, 0:rows - own * chunk, :], chosen_recv.at[iteration, tile])
            value = chosen_in[iteration, tile].astype(F32) - smoothed[tile]
            if last:
                for x in range(G):
                    start = pl.multiple_of(x * PLANE + tile * width, width)
                    potential_ref[:, pl.ds(start, width)] = value[members * x:members * (x + 1), :]
            else:
                raised = jnp.exp(value).astype(BF16)
                depth = pl.ds(pl.multiple_of(tile * width, width), width)
                for target in range(groups):
                    inner = jnp.dot(raised, pair[target, depth, :], preferred_element_type=F32)
                    if step:
                        inner += running[target]
                    if step < groups - 1:
                        running[target] = inner
                    else:
                        columns = slice(target * width, (target + 1) * width)
                        source[:, columns] = (lifted[target] / across(inner)).astype(BF16)

    for _ in range(2 * banks - 1):
        await_bytes(label_out, label_sem.at[0])
    for _ in range(pairs - 1):
        await_bytes(count_out, count_sem.at[0])
    await_bytes(shared_in, shared_sem.at[0])
    for iteration in range(ITERS):
        await_bytes(incoming.at[iteration, :, 0:2 * rows - chunk, :], member_send.at[iteration])
        await_bytes(partial.at[iteration, :, 0:pairs - 1], partial_send.at[iteration])
        await_bytes(chosen.at[iteration, :, 0:2 * rows - chunk, :], chosen_send.at[iteration])


def store_results(centers_in, potential_in, centers_out, potential_out, sems):
    copies = [
        pltpu.make_async_copy(centers_in, centers_out, sems.at[0]),
        pltpu.make_async_copy(potential_in, potential_out, sems.at[1]),
    ]
    for copy in copies:
        copy.start()
    for copy in copies:
        copy.wait()


def fused_device(groups, banks, log_density, assignment):
    members, cells = log_density.shape
    rows, chunk = G * members, G * members // banks
    width = PLANE // groups
    pairs = groups // 2
    kept = G // banks * BARS
    line, pair = host_tables()
    tiled_pair = np.ascontiguousarray(pair.reshape(PLANE, groups, width).transpose(1, 0, 2))
    line_rows = np.kron(line, np.eye(members, dtype=np.float32))
    high = line_rows.astype(ml_dtypes.bfloat16)
    low = (line_rows - high.astype(np.float32)).astype(ml_dtypes.bfloat16)
    line_parts = np.concatenate([high, low, high], axis=1)
    row_scale = np.broadcast_to(1.0 / line_rows.sum(axis=1, keepdims=True), (rows, 128))
    column_scale = (1.0 / pair.astype(np.float32).sum(axis=0)).reshape(PLANE // 128, 128)
    scales = np.concatenate([row_scale, column_scale], axis=0).astype(np.float32)
    operands = (log_density, assignment, jnp.asarray(tiled_pair), jnp.asarray(line_parts), jnp.asarray(scales))
    vmem = pl.BlockSpec(memory_space=pltpu.VMEM)
    dma = pltpu.SemaphoreType.DMA
    results = pl.pallas_call(
        functools.partial(kernel, groups, banks, members),
        out_shape=(
            jax.ShapeDtypeStruct((BARS, cells // banks), BF16),
            jax.ShapeDtypeStruct((members, cells), F32),
        ),
        in_specs=[pl.BlockSpec(memory_space=pltpu.HBM)] * 5,
        out_specs=(vmem, vmem),
        scratch_shapes=[
            pltpu.VMEM(log_density.shape, BF16),
            pltpu.SMEM(assignment.shape, jnp.int32),
            pltpu.VMEM(line_parts.shape, BF16),
            pltpu.VMEM(scales.shape, F32),
            pltpu.VMEM((groups, PLANE, width), BF16),
            pltpu.VMEM((rows, PLANE), BF16),
            pltpu.VMEM((groups, rows, width), F32),
            pltpu.VMEM((groups, rows, width), F32),
            pltpu.VMEM((groups, rows, width), F32),
            pltpu.VMEM((ITERS, groups, rows, width), BF16),
            pltpu.VMEM((ITERS, pairs, 2 * rows, width), BF16),
            pltpu.VMEM((ITERS, pairs, pairs, kept, width), BF16),
            pltpu.VMEM((ITERS, pairs, kept, width), BF16),
            pltpu.VMEM((pairs, kept, width), BF16),
            pltpu.VMEM((ITERS, pairs, 2 * rows, width), BF16),
            pltpu.VMEM((ITERS, groups, rows, width), BF16),
            pltpu.VMEM((2 * rows, 128), BF16),
            pltpu.VMEM((chunk, 128), BF16),
            pltpu.VMEM((BARS, 128), F32),
            pltpu.VMEM((pairs, BARS, 128), F32),
            dma((4 + groups,)), dma((2,)), dma((2,)), dma((2,)),
            dma((ITERS,)), dma((ITERS, pairs)),
            dma((ITERS,)), dma((ITERS, pairs)),
            dma((ITERS,)), dma((ITERS, groups)),
        ],
        compiler_params=pltpu.CompilerParams(
            collective_id=0, has_side_effects=True, vmem_limit_bytes=40 * 1024 * 1024
        ),
    )(*(pltpu.with_memory_space_constraint(operand, pltpu.HBM) for operand in operands))
    pinned = [pltpu.with_memory_space_constraint(result, pltpu.VMEM) for result in results]
    return pl.pallas_call(
        store_results,
        out_shape=tuple(pltpu.HBM(result.shape, result.dtype) for result in results),
        in_specs=[vmem] * 2,
        out_specs=(pl.BlockSpec(memory_space=pltpu.HBM),) * 2,
        scratch_shapes=[dma((2,))],
    )(*pinned)


def log_convolve(field_log, kernel_line, kernel_pair):
    member_count = field_log.shape[0]
    raised = jnp.exp(field_log).astype(BF16).reshape(member_count * G, PLANE)
    inner_sum = jnp.dot(raised, kernel_pair, preferred_element_type=F32).reshape(member_count, G, PLANE)
    outer_sum = jnp.einsum("ij,mjc->mic", kernel_line, inner_sum, precision=lax.Precision.HIGHEST)
    return jnp.log(outer_sum).reshape(member_count, G * PLANE)


def plain_device(log_density, assignment):
    line, pair = host_tables()
    kernel_line, kernel_pair = jnp.asarray(line), jnp.asarray(pair)
    member_count, cell_count = log_density.shape
    row_count = cell_count // 128
    labels = jnp.arange(BARS, dtype=jnp.int32)
    onehot = (assignment[:, None] == labels[None, :]).astype(F32)
    counts = lax.psum(jnp.sum(onehot, axis=0), ("blk", "bank"))
    potential = jnp.zeros((member_count, cell_count), F32)
    center_owned = None
    for _ in range(ITERS):
        source = log_density.astype(F32) - log_convolve(potential, kernel_line, kernel_pair)
        smoothed = log_convolve(source, kernel_line, kernel_pair)
        blocks = smoothed.reshape(member_count, row_count, 128)
        summed = jnp.einsum("mk,mrl->rkl", onehot, blocks, precision=lax.Precision.HIGHEST)
        summed = lax.psum_scatter(summed, "bank", scatter_dimension=0, tiled=True)
        summed = lax.psum(summed, "blk")
        center_owned = (summed / counts[None, :, None]).astype(BF16)
        center_all = lax.all_gather(center_owned, "bank", axis=0, tiled=True)
        chosen = jnp.einsum("mk,rkl->mrl", onehot.astype(BF16), center_all, preferred_element_type=F32)
        potential = chosen.reshape(member_count, cell_count) - smoothed
    centers = jnp.transpose(center_owned, (1, 0, 2)).reshape(BARS, center_owned.shape[0] * 128)
    return centers, potential


def solution(mesh):
    groups, banks = mesh.shape["blk"], mesh.shape["bank"]

    def per_device(log_density, assignment):
        rows = G * log_density.shape[0]
        fits = G % banks == 0 and (rows // banks) % 16 == 0 and PLANE % (128 * groups) == 0
        if fits and groups % 2 == 0 and groups > 2 and banks > 1:
            return fused_device(groups, banks, log_density, assignment)
        return plain_device(log_density, assignment)

    placed = (P(("blk", "bank"), None), P(("blk", "bank")))
    return jax.shard_map(
        per_device,
        mesh=mesh,
        in_specs=placed,
        out_specs=(P(None, "bank"), P(("blk", "bank"), None)),
        check_vma=False,
    )
```
